256 devices in a mesh: bin: 8 (over x, y_hi), nuis: 32 (over z, y_lo, core).
Axes of the slice: x: 4, y: 4 (y_hi: 2, y_lo: 2; y = y_hi * 2 + y_lo), z: 8, core: 2. Of those that a mesh axis runs over, the one named last changes fastest.
Arguments:
- derivative: bfloat16 [16, 4, 4, 8, 3072], P('bin', None, None, None, 'nuis'), may hold values from -6 to 6
- group_ids: int32 [3072], P('nuis'), may hold values from 0 to 7
- group_scale: float32 [8], replicated, may hold values from 0.5 to 2
- plane_coupling: float32 [2, 16], P(None, 'bin'), may hold values from 0.1 to 0.9
- band_second: float32 [3, 4], replicated, may hold values from 0.1 to 1
- band_third: float32 [3, 4], replicated, may hold values from 0.1 to 1
- band_offset: int32 [8], replicated, may hold values from -1 to 1, as said below
- band_width: int32 [8], replicated, may hold values from 1 to 3
- expected: float32 [64, 16, 4, 4, 8], P(None, 'bin'), may hold values from 0.5 to 20
Outputs:
- fisher: float32 [64, 3072, 3072], P('bin', 'nuis')
The draws below stay inside these ranges and needn't reach their ends.
Inputs may be any that keep to these rules, and one draw needn't show every extreme that they name: band_offset + band_width - 1 is at most 1 in every row, so each row reads only its own bin and the two beside it.
All inputs are finite; a program needn't handle non-finite values.
Results may differ from the reference program's by a relative error of at most 0.0026.
Values may be sent and summed in bfloat16 or wider, within the bound.
A program may use at most 64 MiB of HBM per device.

```python
import math
import jax
import jax.numpy as jnp
from jax import lax

P_SIZE = 3072
G = 8
B2 = 4
B3 = 4
B4 = 8
NB1 = 16
K = 64
NBINS = 2048


def band_pair(key):
    key_span, key_offset, key_wide, key_narrow = jax.random.split(jax.random.fold_in(key, 7), 4)
    band_span = jax.random.randint(key_span, (B4,), 1, 4)
    offset = jax.random.randint(key_offset, (B4,), 0, 4 - band_span) - 1
    wide_at = jax.random.randint(key_wide, (), 0, B4)
    narrow_at = (wide_at + jax.random.randint(key_narrow, (), 1, B4)) % B4
    position = jnp.arange(B4)
    band_span = jnp.where(position == wide_at, 3, jnp.where(position == narrow_at, 1, band_span))
    offset = jnp.where(position == wide_at, -1, jnp.where(position == narrow_at, 1, offset))
    return (offset.astype(jnp.int32), band_span.astype(jnp.int32))


def draw_band_offset(key, part):
    return band_pair(key)[0]


def draw_band_width(key, part):
    return band_pair(key)[1]


def touch_ends(entries, rng, low, largest):
    shape = entries.shape
    place = [jax.random.randint(jax.random.fold_in(rng, axis), (), 0, shape[axis]) for axis in range(len(shape))]
    entries = entries.at[tuple(place)].set(low)
    longest = shape.index(max(shape))
    place[longest] = (place[longest] + 1) % shape[longest]
    return entries.at[tuple(place)].set(largest)


def block_levels(stream_key, shape, cuts, low, high):
    loudness = 1.0
    for dim, shards_of in cuts:
        steps = jax.random.uniform(jax.random.fold_in(jax.random.fold_in(stream_key, 6), dim), (shards_of,), jnp.float32, low / len(cuts), high / len(cuts))
        loudness = loudness * jnp.repeat(jnp.exp(steps), shape[dim] // shards_of).reshape((-1,) + (1,) * (len(shape) - 1 - dim))
    return loudness


def bell_draw(own_key, shape, deviation, limit, cuts=(), kind=jnp.bfloat16):
    gain = block_levels(own_key, shape, cuts, -0.22, 0.18) if cuts else 1.0
    values = jax.random.normal(own_key, shape, jnp.float32) * deviation * gain
    return jnp.minimum(jnp.maximum(values, -limit), limit).astype(kind)


def setup_inputs(seed: int = 0) -> dict:
    keys = jax.random.split(jax.random.key(seed), 10)
    return {
        "derivative": bell_draw(keys[0], (NB1, B2, B3, B4, P_SIZE), 1.0, 6.0, ((0, 8), (4, 32))),
        "group_ids": touch_ends(jax.random.randint(keys[1], (P_SIZE,), 0, G), jax.random.fold_in(keys[1], 1), 0, G - 1).astype(jnp.int32),
        "group_scale": jnp.clip(jnp.exp(jax.random.uniform(keys[2], (G,), jnp.float32, math.log(0.5), math.log(2.0))), 0.5, 2.0),
        "plane_coupling": jnp.clip(0.1 + 0.79999997 * jax.random.uniform(keys[3], (2, NB1), jnp.float32) ** block_levels(keys[3], (2, NB1), ((1, 8),), -0.2, 0.2), 0.1, 0.9),
        "band_second": jnp.clip(jax.random.uniform(keys[4], (3, B2), jnp.float32, 0.1, 1.0), 0.1, 1.0),
        "band_third": jnp.clip(jax.random.uniform(keys[5], (3, B3), jnp.float32, 0.1, 1.0), 0.1, 1.0),
        "band_offset": draw_band_offset(jax.random.fold_in(keys[9], 71), 0),
        "band_width": draw_band_width(jax.random.fold_in(keys[9], 71), 0),
        "expected": jnp.clip(jnp.exp(math.log(20.0) - 3.6888795 * jax.random.uniform(keys[8], (K, NB1, B2, B3, B4), jnp.float32) ** block_levels(keys[8], (K, NB1, B2, B3, B4), ((1, 8),), -0.2, 0.2)), 0.5, 20.0),
    }


def banded(band_rows, count):
    row_index = jnp.arange(count)[:, None]
    col_index = jnp.arange(count)[None, :]
    matrix = jnp.where(col_index == row_index - 1, band_rows[0][:, None], jnp.float32(0.0))
    matrix = matrix + jnp.where(col_index == row_index, band_rows[1][:, None], jnp.float32(0.0))
    matrix = matrix + jnp.where(col_index == row_index + 1, band_rows[2][:, None], jnp.float32(0.0))
    return matrix


def local_operator(band_second, band_third, band_offset, band_width):
    second_matrix = banded(band_second, band_second.shape[1])
    third_matrix = banded(band_third, band_third.shape[1])
    count = band_offset.shape[0]
    row_index = jnp.arange(count, dtype=jnp.int32)[:, None]
    col_index = jnp.arange(count, dtype=jnp.int32)[None, :]
    distance = col_index - row_index
    inside = (distance >= band_offset[:, None]) & (distance <= band_offset[:, None] + band_width[:, None] - 1)
    fourth_matrix = jnp.where(inside, 1.0 / band_width[:, None].astype(jnp.float32), jnp.float32(0.0))
    return jnp.kron(second_matrix, jnp.kron(third_matrix, fourth_matrix))


def reference(derivative, group_ids, group_scale, plane_coupling, band_second, band_third, band_offset, band_width, expected):
    column_gain = group_scale[group_ids]
    source = derivative.astype(jnp.float32)
    padded = jnp.pad(source, ((1, 1), (0, 0), (0, 0), (0, 0), (0, 0)))
    lower_side = plane_coupling[0][:, None, None, None, None]
    upper_side = plane_coupling[1][:, None, None, None, None]
    mixed = source + lower_side * padded[:-2] + upper_side * padded[2:]
    operator = local_operator(band_second, band_third, band_offset, band_width)
    cells = B2 * B3 * B4
    flattened = mixed.reshape(NB1, cells, P_SIZE)
    smeared = jnp.einsum("ij,ajc->aic", operator, flattened, precision=lax.Precision.HIGHEST) * column_gain[None, None, :]
    smeared = smeared.reshape(NB1 * cells, P_SIZE).astype(jnp.bfloat16)
    inverse = (1.0 / expected.reshape(K, NB1 * cells)) / NBINS

    def one_point(inverse_row):
        weighted = (smeared.astype(jnp.float32) * inverse_row[:, None]).astype(jnp.bfloat16)
        return jnp.dot(weighted.T, smeared, preferred_element_type=jnp.float32)

    return lax.map(one_point, inverse)
```

```python
import functools

import jax
import jax.numpy as jnp
from jax import lax
from jax.experimental import pallas as pl
from jax.experimental.pallas import tpu as pltpu
from jax.sharding import PartitionSpec as P

MESH = pl.DeviceIdType.MESH
NT = (((1,), (1,)), ((), ()))
CELLS = 128
OWN = 96
ROWS = 256
SLOT = {0: 0, 1: 1, -1: 2, 2: 3, -2: 4, 3: 5, -3: 6, 4: 7, -4: 7}
DISTANCE = (0, 1, -1, 2, -2, 3, -3, 4)
GROUPS = ((0, 1), (1, 2), (3, 2), (5, 2), (7, 1))
PART = {"A": (0, 32), "B": (32, 32), "C": (64, 32), "BC": (32, 64)}


def names():
    out = ["halo+", "halo-"]
    out += [f"exp{o}" for o in range(1, 8)]
    out += [f"ap{dx}{dy}" for dx in range(4) for dy in range(4) if dx or dy]
    out += [f"z{s}{w}" for s in range(1, 5) for w in "+-"]
    for s in range(1, 5):
        for w in "+-":
            for h in range(2):
                if s < 4 or h == (0 if w == "+" else 1):
                    out.append(f"az{s}{w}{h}")
    for g in range(5):
        out += [f"by{g}{d}" for d in range(1, 4)] + [f"cx{g}{d}" for d in range(1, 4)]
        out += [f"{n}{g}{w}" for n in ("bx", "bf", "cy", "cf") for w in "+-"]
        out += [f"core{p}{g}" for p in "ABC"]
    return {n: i for i, n in enumerate(out)}


NAMES = names()


def kernel(
    deriv_ref,
    ids_ref,
    scale_ref,
    coupling_ref,
    second_ref,
    third_ref,
    offset_ref,
    width_ref,
    exp_ref,
    out_ref,
    panels,
    weights,
    halo,
    expected,
    send_sem,
    recv_sem,
):
    b = lax.axis_index("bin")
    n = lax.axis_index("nuis")
    x, yh = b // 2, b % 2
    z, yl, c = n // 4, (n // 2) % 2, n % 2
    y = yh * 2 + yl

    def device(dx=0, dy=0, dz=0, dc=0):
        nx, ny, nz = (x + dx + 4) % 4, (y + dy + 4) % 4, (z + dz + 8) % 8
        nc = (c + dc) % 2
        return (nx * 2 + ny // 2, (nz * 2 + ny % 2) * 2 + nc)

    partners = [dict(dx=dx, dy=dy) for dx in range(4) for dy in range(4) if dx or dy]
    partners += [dict(dz=1), dict(dz=-1), dict(dc=1)]
    barrier = pltpu.get_barrier_semaphore()
    for p in partners:
        pl.semaphore_signal(barrier, inc=1, device_id=device(**p), device_id_type=MESH)
    pl.semaphore_wait(barrier, len(partners))

    started = {}
    arrived = set()

    def send(name, src, dst, target):
        i = NAMES[name]
        copy = pltpu.make_async_remote_copy(
            src_ref=src,
            dst_ref=dst,
            send_sem=send_sem.at[i],
            recv_sem=recv_sem.at[i],
            device_id=target,
            device_id_type=MESH,
        )
        copy.start()
        started[name] = copy

    def need(*events):
        for e in events:
            if e not in arrived:
                started[e].wait_recv()
                arrived.add(e)

    nb, pb = (b + 1) % 8, (b + 7) % 8
    send("halo+", deriv_ref.at[pl.ds(CELLS, CELLS)], halo.at[0], (nb, n))
    send("halo-", deriv_ref.at[pl.ds(0, CELLS)], halo.at[1], (pb, n))
    for o in range(1, 8):
        peer = (b + o) % 8
        send(
            f"exp{o}",
            exp_ref.at[pl.ds(pl.multiple_of(peer * 8, 8), 8)],
            expected.at[b],
            (peer, n),
        )
    expected[b] = exp_ref[pl.ds(pl.multiple_of(b * 8, 8), 8), :]

    row = lax.broadcasted_iota(jnp.int32, (CELLS, CELLS), 0)
    col = lax.broadcasted_iota(jnp.int32, (CELLS, CELLS), 1)
    zero = jnp.zeros((CELLS, CELLS), jnp.float32)

    def chain(index, values):
        out = jnp.full((CELLS, CELLS), values[-1])
        for i in range(len(values) - 2, -1, -1):
            out = jnp.where(index == i, values[i], out)
        return out

    def banded(ref, i, j):
        out = zero
        for d in range(3):
            out = jnp.where(j - i == d - 1, chain(i, [ref[d, t] for t in range(4)]), out)
        return out

    r4, c4 = row % 8, col % 8
    offset = chain(r4, [offset_ref[t] for t in range(8)])
    width = chain(r4, [width_ref[t] for t in range(8)])
    inside = (c4 - r4 >= offset) & (c4 - r4 <= offset + width - 1)
    fourth = jnp.where(inside, 1.0 / width.astype(jnp.float32), zero)
    operator = (
        banded(second_ref, row // 32, col // 32)
        * (banded(third_ref, (row // 8) % 4, (col // 8) % 4) * fourth)
    )
    ids = ids_ref[...]
    gain = jnp.zeros((1, OWN), jnp.float32)
    for g in range(8):
        gain = jnp.where(ids == g, scale_ref[g], gain)
    first = deriv_ref[pl.ds(0, CELLS), :].astype(jnp.float32)
    second = deriv_ref[pl.ds(CELLS, CELLS), :].astype(jnp.float32)
    low0 = jnp.where(b == 0, 0.0, coupling_ref[0, 0])
    high1 = jnp.where(b == 7, 0.0, coupling_ref[1, 1])

    need("halo+", "halo-")
    below = halo[0].astype(jnp.float32)
    above = halo[1].astype(jnp.float32)
    mixed = (
        first + low0 * below + coupling_ref[1, 0] * second,
        second + coupling_ref[0, 1] * first + high1 * above,
    )
    for a in range(2):
        panel = lax.dot_general(
            operator,
            mixed[a] * gain,
            (((1,), (0,)), ((), ())),
            precision=lax.Precision.HIGHEST,
            preferred_element_type=jnp.float32,
        )
        panels[0, x, yh, yl, c, :, a * CELLS : (a + 1) * CELLS] = panel.T.astype(jnp.bfloat16)

    def own(slots, part, *place):
        lo, size = PART[part]
        return panels.at[(slots, *place, pl.ds(lo, size))]

    def z_step(s):
        for w, sign in (("+", 1), ("-", -1)):
            if s > 1:
                need(f"z{s - 1}{w}")
            part = "BC" if s < 4 else ("B" if sign == 1 else "C")
            src = SLOT[-sign * (s - 1)]
            dst = SLOT[-sign * s]
            send(
                f"z{s}{w}",
                own(src, part, x, yh, yl, c),
                own(dst, part, x, yh, yl, c),
                device(dz=sign),
            )

    def group(g):
        return pl.ds(*GROUPS[g])

    def group_here(g):
        if 1 <= g:
            need(f"z{g}+", f"z{g}-")

    def first_axis(g):
        group_here(g)
        mine_b = own(group(g), "B", x, yh, yl, c)
        mine_c = own(group(g), "C", x, yh, yl, c)
        for d in (1, 3, 2):
            send(f"by{g}{d}", mine_b, mine_b, device(dy=d))
            send(f"cx{g}{d}", mine_c, mine_c, device(dx=d))

    def second_axis(g):
        need(*[f"by{g}{d}" for d in (1, 3, 2)])
        line = own(group(g), "B", x, slice(None), slice(None), c)
        for w, sign in (("+", 1), ("-", -1)):
            send(f"bx{g}{w}", line, line, device(dx=sign))
        need(*[f"cx{g}{d}" for d in (1, 3, 2)])
        line = own(group(g), "C", slice(None), yh, yl, c)
        for w, sign in (("+", 1), ("-", -1)):
            send(f"cy{g}{w}", line, line, device(dy=sign))

    def far(g):
        for w, sign in (("+", 1), ("-", -1)):
            need(f"bx{g}{w}")
            line = own(group(g), "B", (x - sign + 4) % 4, 0 if sign == 1 else 1, slice(None), c)
            send(f"bf{g}{w}", line, line, device(dx=sign))
        for w, sign in (("+", 1), ("-", -1)):
            need(f"cy{g}{w}")
            oy = (y - sign + 4) % 4
            line = own(group(g), "C", pl.ds(0 if sign == 1 else 2, 2), oy // 2, oy % 2, c)
            send(f"cf{g}{w}", line, line, device(dy=sign))

    def plane_a():
        mine = own(0, "A", x, yh, yl, c)
        for dx in range(4):
            for dy in range(4):
                if dx or dy:
                    send(f"ap{dx}{dy}", mine, mine, device(dx=dx, dy=dy))

    def ring_a(s):
        for h in range(2):
            for w, sign in (("+", 1), ("-", -1)):
                if f"az{s}{w}{h}" not in NAMES:
                    continue
                if s > 1:
                    need(f"az{s - 1}{w}{h}")
                else:
                    need(*[f"ap{dx}{dy}" for dx in range(4) for dy in range(4) if dx or dy])
                place = (pl.ds(2 * h, 2), slice(None), slice(None), c)
                send(
                    f"az{s}{w}{h}",
                    own(SLOT[-sign * (s - 1)], "A", *place),
                    own(SLOT[-sign * s], "A", *place),
                    device(dz=sign),
                )

    def own_a(g):
        if g == 0:
            need(*[f"ap{dx}{dy}" for dx in range(4) for dy in range(4) if dx or dy])
        else:
            need(*[e for e in NAMES if e.startswith(f"az{g}")])

    def share_bc(g):
        need(*[f"bf{g}{w}" for w in "+-"])
        block = own(group(g), "B", slice(None), slice(None), slice(None), c)
        send(f"coreB{g}", block, block, device(dc=1))
        need(*[f"cf{g}{w}" for w in "+-"])
        block = own(group(g), "C", slice(None), slice(None), slice(None), c)
        send(f"coreC{g}", block, block, device(dc=1))

    def share_a(g):
        own_a(g)
        block = own(group(g), "A", slice(None), slice(None), slice(None), c)
        send(f"coreA{g}", block, block, device(dc=1))

    def weigh():
        need(*[f"exp{o}" for o in range(1, 8)])

        def body(t, _):
            inverse = 1.0 / expected[t] / (8.0 * ROWS)
            mine = panels[0, t // 2, t % 2, yl, c].astype(jnp.float32)
            for k in range(8):
                weights[t, pl.ds(k * OWN, OWN), :] = (mine * inverse[k : k + 1, :]).astype(
                    jnp.bfloat16
                )
            return 0

        lax.fori_loop(0, 8, body, 0)

    def multiply(g):
        need(f"coreA{g}", f"coreB{g}", f"coreC{g}")
        start, count = GROUPS[g]
        lhs = jnp.concatenate([weights[t] for t in range(8)], axis=1)
        blocks = []
        for i in range(count):
            blocks.append(
                jnp.concatenate(
                    [panels[start + i, t // 2, t % 2].reshape(4 * OWN, ROWS) for t in range(8)], axis=1
                )
            )
        rhs = blocks[0] if count == 1 else jnp.concatenate(blocks, axis=0)
        step = 384 if count == 1 else 256
        for i in range(count * 384 // step):
            product = lax.dot_general(
                lhs, rhs[i * step : (i + 1) * step], NT, preferred_element_type=jnp.float32
            )
            at = i * step
            while at < (i + 1) * step:
                which, inner = at // 384, at % 384
                size = min(384 - inner, (i + 1) * step - at)
                zz = (z + DISTANCE[start + which] + 8) % 8
                column = pl.multiple_of(zz * 384 + inner, 128)
                out_ref[:, pl.ds(column, size)] = product[:, at - i * step : at - i * step + size]
                at += size

    z_step(1)
    first_axis(0)
    plane_a()
    z_step(2)
    first_axis(1)
    second_axis(0)
    z_step(3)
    first_axis(2)
    ring_a(1)
    far(0)
    second_axis(1)
    share_a(0)
    z_step(4)
    first_axis(3)
    share_bc(0)
    far(1)
    first_axis(4)
    second_axis(2)
    weigh()
    multiply(0)
    ring_a(2)
    share_a(1)
    second_axis(3)
    share_bc(1)
    far(2)
    multiply(1)
    ring_a(3)
    share_a(2)
    second_axis(4)
    share_bc(2)
    far(3)
    multiply(2)
    ring_a(4)
    share_a(3)
    far(4)
    share_bc(3)
    multiply(3)
    share_bc(4)
    share_a(4)
    multiply(4)
    for copy in started.values():
        copy.wait_send()


def local(
    derivative,
    group_ids,
    group_scale,
    plane_coupling,
    band_second,
    band_third,
    band_offset,
    band_width,
    expected,
):
    flat = derivative.reshape(2 * CELLS, OWN)
    every = expected.reshape(64, ROWS)
    smem = pl.BlockSpec(memory_space=pltpu.SMEM)
    vmem = pl.BlockSpec(memory_space=pltpu.VMEM)
    count = len(NAMES)
    out = pl.pallas_call(
        kernel,
        out_shape=jax.ShapeDtypeStruct((8 * OWN, 3072), jnp.float32),
        in_specs=[vmem, vmem, smem, smem, smem, smem, smem, smem, vmem],
        out_specs=vmem,
        scratch_shapes=[
            pltpu.VMEM((8, 4, 2, 2, 2, OWN, ROWS), jnp.bfloat16),
            pltpu.VMEM((8, 8 * OWN, ROWS), jnp.bfloat16),
            pltpu.VMEM((2, CELLS, OWN), jnp.bfloat16),
            pltpu.VMEM((8, 8, ROWS), jnp.float32),
            pltpu.SemaphoreType.DMA((count,)),
            pltpu.SemaphoreType.DMA((count,)),
        ],
        compiler_params=pltpu.CompilerParams(
            collective_id=0, has_side_effects=True, vmem_limit_bytes=40 * 1024 * 1024
        ),
        cost_estimate=pl.CostEstimate(
            flops=2 * 768 * 2048 * 3072, bytes_accessed=10_000_000, transcendentals=0
        ),
        name="fisher",
    )(
        flat,
        group_ids.reshape(1, OWN),
        group_scale,
        plane_coupling,
        band_second,
        band_third,
        band_offset,
        band_width,
        every,
    )
    return out.reshape(8, OWN, 3072)


def solution(mesh):
    placed = (
        P("bin", None, None, None, "nuis"),
        P("nuis"),
        P(),
        P(None, "bin"),
        P(),
        P(),
        P(),
        P(),
        P(None, "bin", None, None, None),
    )
    return jax.shard_map(
        local, mesh=mesh, in_specs=placed, out_specs=P("bin", "nuis", None), check_vma=False
    )
```

```python
import functools

import jax
import jax.numpy as jnp
from jax import lax
from jax.experimental import pallas as pl
from jax.experimental.pallas import tpu as pltpu
from jax.sharding import PartitionSpec as P

MESH = pl.DeviceIdType.MESH
NT = (((1,), (1,)), ((), ()))
CELLS = 128
OWN = 96
ROWS = 256
SLOT = {0: 0, 1: 1, -1: 2, 2: 3, -2: 4, 3: 5, -3: 6, 4: 7, -4: 7}
DISTANCE = (0, 1, -1, 2, -2, 3, -3, 4)
GROUPS = ((0, 1), (1, 2), (3, 2), (5, 2), (7, 1))
GROUP_OF = (0, 1, 1, 2, 2, 3, 3, 4)
WIDE = 512
PART = {"A": (0, 32), "B": (32, 32), "C": (64, 32), "BC": (32, 64)}


HEAD = 1536


def events():
    out = ["halo+", "halo-", "exp", "ap"]
    out += [f"z{s}{w}" for s in range(1, 5) for w in "+-"]
    for s in range(1, 5):
        for w in "+-":
            for h in range(2):
                if s < 4 or h == (0 if w == "+" else 1):
                    out.append(f"az{s}{w}{h}")
    for g in range(5):
        out += [f"by{g}", f"cx{g}", f"bf{g}", f"cf{g}"]
        out += [f"{n}{g}{w}" for n in ("bx", "cy") for w in "+-"]
        out += [f"core{p}{g}" for p in "ABC"]
    return {n: i for i, n in enumerate(out)}


EVENTS = events()
DEPARTURES = ["halo+", "halo-", "exp", "ap", "z", "az"]
DEPARTURES += [f"{n}{g}" for n in ("link", "core") for g in range(5)]
DEPARTURES = {n: i for i, n in enumerate(DEPARTURES)}


def slots(i):
    out, at, end = {}, i * WIDE, (i + 1) * WIDE
    while at < end:
        slot, inner = at // 384, at % 384
        out[slot] = (inner, min(384 - inner, end - at))
        at += out[slot][1]
    return out


def product(weights, panels, i):
    lhs = jnp.concatenate([weights[t] for t in range(8)], axis=1)
    blocks = []
    for slot, (inner, size) in slots(i).items():
        block = [panels[slot, t // 2, t % 2].reshape(4 * OWN, ROWS) for t in range(8)]
        blocks.append(jnp.concatenate(block, axis=1)[inner : inner + size])
    return lax.dot_general(
        lhs, jnp.concatenate(blocks, axis=0), NT, preferred_element_type=jnp.float32
    )


def finish(panels, weights, head, out_ref, tail, sems):
    z = lax.div(lax.axis_index("nuis"), 4)
    copies = []

    def write(i, source, first):
        at = first
        for slot, (inner, size) in slots(i).items():
            column = lax.rem(z + (DISTANCE[slot] + 8), 8) * 384 + inner
            copy = pltpu.make_async_copy(
                source.at[:, pl.ds(at, size)],
                out_ref.at[:, pl.ds(pl.multiple_of(column, 128), size)],
                sems.at[len(copies)],
            )
            copy.start()
            copies.append(copy)
            at += size

    for i in range(6):
        if i < HEAD // WIDE:
            write(i, head, i * WIDE)
        else:
            tail[:, i * WIDE - HEAD : (i + 1) * WIDE - HEAD] = product(weights, panels, i)
            write(i, tail, i * WIDE - HEAD)
    for copy in copies:
        copy.wait()


def kernel(
    deriv_in,
    ids_in,
    scale_in,
    coupling_in,
    second_in,
    third_in,
    offset_in,
    width_in,
    exp_in,
    panels,
    weights,
    out_ref,
    halo,
    expected,
    deriv_ref,
    ids_ref,
    scale_ref,
    coupling_ref,
    second_ref,
    third_ref,
    offset_ref,
    width_ref,
    exp_cols,
    exp_ref,
    operator_ref,
    gain_ref,
    in_sem,
    send_sem,
    recv_sem,
):
    b = lax.axis_index("bin")
    n = lax.axis_index("nuis")
    x, yh = lax.div(b, 2), lax.rem(b, 2)
    z, yl, c = lax.div(n, 4), lax.rem(lax.div(n, 2), 2), lax.rem(n, 2)
    y = yh * 2 + yl

    def device(dx=0, dy=0, dz=0, dc=0):
        nx = lax.rem(x + (dx + 4), 4) if dx else x
        ny = lax.rem(y + (dy + 4), 4) if dy else y
        nz = lax.rem(z + (dz + 8), 8) if dz else z
        nc = 1 - c if dc else c
        nyh, nyl = (lax.div(ny, 2), lax.rem(ny, 2)) if dy else (yh, yl)
        return (nx * 2 + nyh, nz * 4 + nyl * 2 + nc)

    inputs = [
        pltpu.make_async_copy(src, dst, in_sem.at[i])
        for i, (src, dst) in enumerate(
            (
                (second_in, second_ref),
                (third_in, third_ref),
                (offset_in, offset_ref),
                (width_in, width_ref),
                (scale_in, scale_ref),
                (ids_in, ids_ref),
                (coupling_in, coupling_ref),
                (exp_in, exp_cols),
                (deriv_in, deriv_ref),
            )
        )
    ]
    for copy in inputs:
        copy.start()

    partners = [dict(dx=dx, dy=dy) for dx in range(4) for dy in range(4) if dx or dy]
    partners += [dict(dz=1), dict(dz=-1), dict(dc=1)]
    barrier = pltpu.get_barrier_semaphore()
    for p in partners:
        pl.semaphore_signal(barrier, inc=1, device_id=device(**p), device_id_type=MESH)

    for copy in inputs[:6]:
        copy.wait()
    row = lax.broadcasted_iota(jnp.int32, (CELLS, CELLS), 0)
    col = lax.broadcasted_iota(jnp.int32, (CELLS, CELLS), 1)
    zero = jnp.zeros((CELLS, CELLS), jnp.float32)

    def chain(index, values):
        out = jnp.full((CELLS, CELLS), values[-1])
        for i in range(len(values) - 2, -1, -1):
            out = jnp.where(index == i, values[i], out)
        return out

    def banded(ref, i, j):
        out = zero
        for d in range(3):
            out = jnp.where(j - i == d - 1, chain(i, [ref[d, t] for t in range(4)]), out)
        return out

    r4, c4 = row & 7, col & 7
    offset = chain(r4, [offset_ref[t] for t in range(8)])
    width = chain(r4, [width_ref[t] for t in range(8)])
    inside = (c4 - r4 >= offset) & (c4 - r4 <= offset + width - 1)
    fourth = jnp.where(inside, 1.0 / width.astype(jnp.float32), zero)
    operator_ref[...] = (
        banded(second_ref, row >> 5, col >> 5)
        * (banded(third_ref, (row >> 3) & 3, (col >> 3) & 3) * fourth)
    )
    ids = ids_ref[...]
    gain = jnp.zeros((1, OWN), jnp.float32)
    for g in range(8):
        gain = jnp.where(ids == g, scale_ref[g], gain)
    gain_ref[...] = gain
    for copy in inputs[6:]:
        copy.wait()
    exp_ref[...] = exp_cols[...].T
    pl.semaphore_wait(barrier, len(partners))

    started = {}
    departed = {}
    arrived = set()

    def rows(count, wide=1):
        return weights.at[pl.ds(0, wide), pl.ds(0, count)]

    def send(event, departure, src, dst, target):
        copy = pltpu.make_async_remote_copy(
            src_ref=src,
            dst_ref=dst,
            send_sem=send_sem.at[DEPARTURES[departure]],
            recv_sem=recv_sem.at[EVENTS[event]],
            device_id=target,
            device_id_type=MESH,
        )
        copy.start()
        started[event] = copy
        departed[departure] = copy

    def empty(semaphore, like):
        pltpu.make_async_copy(like, like, semaphore).wait()

    def need(*events):
        for e in events:
            if e in arrived:
                continue
            arrived.add(e)
            semaphore = recv_sem.at[EVENTS[e]]
            if e == "exp":
                empty(semaphore, expected.at[pl.ds(0, 7)])
            elif e == "ap":
                empty(semaphore, rows(480))
            elif e[:2] in ("by", "cx"):
                empty(semaphore, rows(96 * GROUPS[int(e[2])][1]))
            elif e[:2] in ("bf", "cf"):
                empty(semaphore, rows(128 * GROUPS[int(e[2])][1]))
            else:
                started[e].wait_recv()

    nb, pb = lax.rem(b + 1, 8), lax.rem(b + 7, 8)
    send("halo+", "halo+", deriv_ref.at[pl.ds(CELLS, CELLS)], halo.at[0], (nb, n))
    send("halo-", "halo-", deriv_ref.at[pl.ds(0, CELLS)], halo.at[1], (pb, n))
    first = deriv_ref[pl.ds(0, CELLS), :].astype(jnp.float32)
    second = deriv_ref[pl.ds(CELLS, CELLS), :].astype(jnp.float32)
    low0 = jnp.where(b == 0, 0.0, coupling_ref[0, 0])
    high1 = jnp.where(b == 7, 0.0, coupling_ref[1, 1])

    need("halo+", "halo-")
    below = halo[0].astype(jnp.float32)
    above = halo[1].astype(jnp.float32)
    mixed = (
        first + low0 * below + coupling_ref[1, 0] * second,
        second + coupling_ref[0, 1] * first + high1 * above,
    )
    for a in range(2):
        panel = lax.dot_general(
            operator_ref[...],
            mixed[a] * gain_ref[...],
            (((1,), (0,)), ((), ())),
            precision=lax.Precision.HIGHEST,
            preferred_element_type=jnp.float32,
        )
        panels[0, x, yh, yl, c, :, a * CELLS : (a + 1) * CELLS] = panel.T.astype(jnp.bfloat16)

    def send_expected():
        for o in range(1, 8):
            peer = lax.rem(b + o, 8)
            send(
                "exp",
                "exp",
                exp_ref.at[pl.ds(pl.multiple_of(peer * 8, 8), 8)],
                expected.at[b],
                (peer, n),
            )
        expected[b] = exp_ref[pl.ds(pl.multiple_of(b * 8, 8), 8), :]

    def own(slots, part, *place):
        lo, size = PART[part]
        return panels.at[(slots, *place, pl.ds(lo, size))]

    def z_step(s):
        for w, sign in (("+", 1), ("-", -1)):
            if s > 1:
                need(f"z{s - 1}{w}")
            part = "BC" if s < 4 else ("B" if sign == 1 else "C")
            src = SLOT[-sign * (s - 1)]
            dst = SLOT[-sign * s]
            send(
                f"z{s}{w}",
                "z",
                own(src, part, x, yh, yl, c),
                own(dst, part, x, yh, yl, c),
                device(dz=sign),
            )

    def group(g):
        return pl.ds(*GROUPS[g])

    def group_here(g):
        if 1 <= g:
            need(f"z{g}+", f"z{g}-")

    def first_axis(g):
        group_here(g)
        mine_b = own(group(g), "B", x, yh, yl, c)
        mine_c = own(group(g), "C", x, yh, yl, c)
        for d in (1, 3, 2):
            send(f"by{g}", f"link{g}", mine_b, mine_b, device(dy=d))
            send(f"cx{g}", f"link{g}", mine_c, mine_c, device(dx=d))

    def second_axis(g):
        need(f"by{g}")
        line = own(group(g), "B", x, slice(None), slice(None), c)
        for w, sign in (("+", 1), ("-", -1)):
            send(f"bx{g}{w}", f"link{g}", line, line, device(dx=sign))
        need(f"cx{g}")
        line = own(group(g), "C", slice(None), yh, yl, c)
        for w, sign in (("+", 1), ("-", -1)):
            send(f"cy{g}{w}", f"link{g}", line, line, device(dy=sign))

    def far(g):
        for w, sign in (("+", 1), ("-", -1)):
            need(f"bx{g}{w}")
            line = own(group(g), "B", lax.rem(x + (4 - sign), 4), 0 if sign == 1 else 1, slice(None), c)
            send(f"bf{g}", f"link{g}", line, line, device(dx=sign))
        for w, sign in (("+", 1), ("-", -1)):
            need(f"cy{g}{w}")
            oy = lax.rem(y + (4 - sign), 4)
            line = own(group(g), "C", pl.ds(0 if sign == 1 else 2, 2), lax.div(oy, 2), lax.rem(oy, 2), c)
            send(f"cf{g}", f"link{g}", line, line, device(dy=sign))

    def plane_a():
        mine = own(0, "A", x, yh, yl, c)
        for dx in range(4):
            for dy in range(4):
                if dx or dy:
                    send("ap", "ap", mine, mine, device(dx=dx, dy=dy))

    def ring_a(s, h):
        for w, sign in (("+", 1), ("-", -1)):
            if f"az{s}{w}{h}" not in EVENTS:
                continue
            if s > 1:
                need(f"az{s - 1}{w}{h}")
            else:
                need("ap")
            place = (pl.ds(2 * h, 2), slice(None), slice(None), c)
            send(
                f"az{s}{w}{h}",
                "az",
                own(SLOT[-sign * (s - 1)], "A", *place),
                own(SLOT[-sign * s], "A", *place),
                device(dz=sign),
            )

    def own_a(g):
        if g == 0:
            need("ap")
        else:
            need(*[e for e in EVENTS if e.startswith(f"az{g}")])

    def share_bc(g):
        need(f"bf{g}")
        block = own(group(g), "B", slice(None), slice(None), slice(None), c)
        send(f"coreB{g}", f"core{g}", block, block, device(dc=1))
        need(f"cf{g}")
        block = own(group(g), "C", slice(None), slice(None), slice(None), c)
        send(f"coreC{g}", f"core{g}", block, block, device(dc=1))

    def share_a(g):
        own_a(g)
        block = own(group(g), "A", slice(None), slice(None), slice(None), c)
        send(f"coreA{g}", f"core{g}", block, block, device(dc=1))

    def weigh():
        need("exp")

        def body(t, _):
            inverse = 1.0 / expected[t] / (8.0 * ROWS)
            mine = panels[0, lax.div(t, 2), lax.rem(t, 2), yl, c].astype(jnp.float32)
            for k in range(8):
                weights[t, pl.ds(k * OWN, OWN), :] = (mine * inverse[k : k + 1, :]).astype(
                    jnp.bfloat16
                )
            return 0

        lax.fori_loop(0, 8, body, 0)

    def multiply(i):
        for slot in slots(i):
            need(*[f"core{p}{GROUP_OF[slot]}" for p in "ABC"])
        out_ref[:, i * WIDE : (i + 1) * WIDE] = product(weights, panels, i)

    z_step(1)
    first_axis(0)
    plane_a()
    z_step(2)
    first_axis(1)
    second_axis(0)
    z_step(3)
    ring_a(1, 0)
    first_axis(2)
    ring_a(1, 1)
    second_axis(1)
    far(0)
    send_expected()
    z_step(4)
    first_axis(3)
    share_a(0)
    second_axis(2)
    far(1)
    ring_a(2, 0)
    first_axis(4)
    second_axis(3)
    share_bc(0)
    ring_a(2, 1)
    weigh()
    share_a(1)
    far(2)
    second_axis(4)
    ring_a(3, 0)
    share_bc(1)
    ring_a(3, 1)
    far(3)
    multiply(0)
    share_a(2)
    ring_a(4, 0)
    share_bc(2)
    far(4)
    multiply(1)
    ring_a(4, 1)
    share_a(3)
    share_bc(3)
    multiply(2)
    share_bc(4)
    share_a(4)
    for g in range(5):
        need(*[f"core{p}{g}" for p in "ABC"])
    for d in DEPARTURES:
        semaphore = send_sem.at[DEPARTURES[d]]
        if d == "exp":
            empty(semaphore, expected.at[pl.ds(0, 7)])
        elif d == "ap":
            empty(semaphore, rows(480))
        elif d == "z":
            empty(semaphore, rows(448))
        elif d == "az":
            empty(semaphore, rows(512, 7))
        elif d.startswith("link"):
            empty(semaphore, rows(480, 2 * GROUPS[int(d[4])][1]))
        elif d.startswith("core"):
            empty(semaphore, panels.at[group(int(d[4])), :, :, :, 0])
        else:
            departed[d].wait_send()


def local(
    derivative,
    group_ids,
    group_scale,
    plane_coupling,
    band_second,
    band_third,
    band_offset,
    band_width,
    expected,
):
    flat = derivative.reshape(2 * CELLS, OWN)
    every = expected.transpose(1, 2, 3, 4, 0).reshape(ROWS, 64)
    hbm = pl.BlockSpec(memory_space=pltpu.HBM)
    vmem = pl.BlockSpec(memory_space=pltpu.VMEM)
    made = pl.pallas_call(
        kernel,
        out_shape=[
            pltpu.VMEM((8, 4, 2, 2, 2, OWN, ROWS), jnp.bfloat16),
            pltpu.VMEM((8, 8 * OWN, ROWS), jnp.bfloat16),
            pltpu.VMEM((8 * OWN, HEAD), jnp.float32),
        ],
        in_specs=[hbm] * 9,
        out_specs=[vmem] * 3,
        scratch_shapes=[
            pltpu.VMEM((2, CELLS, OWN), jnp.bfloat16),
            pltpu.VMEM((8, 8, ROWS), jnp.float32),
            pltpu.VMEM((2 * CELLS, OWN), jnp.bfloat16),
            pltpu.VMEM((1, OWN), jnp.int32),
            pltpu.SMEM((8,), jnp.float32),
            pltpu.SMEM((2, 2), jnp.float32),
            pltpu.SMEM((3, 4), jnp.float32),
            pltpu.SMEM((3, 4), jnp.float32),
            pltpu.SMEM((8,), jnp.int32),
            pltpu.SMEM((8,), jnp.int32),
            pltpu.VMEM((ROWS, 64), jnp.float32),
            pltpu.VMEM((64, ROWS), jnp.float32),
            pltpu.VMEM((CELLS, CELLS), jnp.float32),
            pltpu.VMEM((1, OWN), jnp.float32),
            pltpu.SemaphoreType.DMA((9,)),
            pltpu.SemaphoreType.DMA((len(DEPARTURES),)),
            pltpu.SemaphoreType.DMA((len(EVENTS),)),
        ],
        compiler_params=pltpu.CompilerParams(
            collective_id=0, has_side_effects=True, vmem_limit_bytes=16 * 1024 * 1024
        ),
        cost_estimate=pl.CostEstimate(
            flops=2 * 768 * 2048 * HEAD, bytes_accessed=10_000_000, transcendentals=0
        ),
        name="fisher",
    )(
        *[
            pltpu.with_memory_space_constraint(a, pltpu.HBM)
            for a in (
                flat,
                group_ids.reshape(1, OWN),
                group_scale,
                plane_coupling,
                band_second,
                band_third,
                band_offset,
                band_width,
                every,
            )
        ]
    )
    out = pl.pallas_call(
        finish,
        out_shape=jax.ShapeDtypeStruct((8 * OWN, 3072), jnp.float32),
        in_specs=[vmem] * 3,
        out_specs=hbm,
        scratch_shapes=[
            pltpu.VMEM((8 * OWN, 3072 - HEAD), jnp.float32),
            pltpu.SemaphoreType.DMA((16,)),
        ],
        compiler_params=pltpu.CompilerParams(vmem_limit_bytes=16 * 1024 * 1024),
        cost_estimate=pl.CostEstimate(
            flops=2 * 768 * 2048 * (3072 - HEAD), bytes_accessed=10_000_000, transcendentals=0
        ),
        name="finish",
    )(*[pltpu.with_memory_space_constraint(a, pltpu.VMEM) for a in made])
    return out.reshape(8, OWN, 3072)


def solution(mesh):
    placed = (
        P("bin", None, None, None, "nuis"),
        P("nuis"),
        P(),
        P(None, "bin"),
        P(),
        P(),
        P(),
        P(),
        P(None, "bin", None, None, None),
    )
    return jax.shard_map(
        local, mesh=mesh, in_specs=placed, out_specs=P("bin", "nuis", None), check_vma=False
    )
```

```python
import functools

import jax
import jax.numpy as jnp
from jax import lax
from jax.experimental import pallas as pl
from jax.experimental.pallas import tpu as pltpu
from jax.sharding import PartitionSpec as P

MESH = pl.DeviceIdType.MESH
NT = (((1,), (1,)), ((), ()))
CELLS = 128
OWN = 96
ROWS = 256
SLOT = {0: 0, 1: 1, -1: 2, 2: 3, -2: 4, 3: 5, -3: 6, 4: 7, -4: 7}
DISTANCE = (0, 1, -1, 2, -2, 3, -3, 4)
GROUPS = ((0, 1), (1, 2), (3, 2), (5, 2), (7, 1))
GROUP_OF = (0, 1, 1, 2, 2, 3, 3, 4)
WIDE = 512
PART = {"A": (0, 32),  "B": (32, 32), "C": (64, 32), "BC": (32, 64)}


HEAD = 2048


def events():
    out = ["halo+", "halo-", "exp", "ap"]
    out += [f"z{s}{w}" for s in range(1, 5) for w in "+-"]
    for s in range(1, 5):
        for w in "+-":
            for h in range(2):
                if s < 4 or h == (0 if w == "+" else 1):
                    out.append(f"az{s}{w}{h}")
    for g in range(5):
        out += [f"by{g}", f"cx{g}", f"bf{g}", f"cf{g}"]
        out += [f"{n}{g}{w}" for n in ("bx", "cy") for w in "+-"]
        out += [f"core{p}{g}" for p in "ANF"]
    return {n: i for i, n in enumerate(out)}


EVENTS = events()
DEPARTURES = ["halo+", "halo-", "exp", "ap", "z", "az"]
DEPARTURES += [f"{n}{g}" for n in ("link", "core") for g in range(5)]
DEPARTURES = {n: i for i, n in enumerate(DEPARTURES)}


def slots(i):
    out, at, end = {}, i * WIDE, (i + 1) * WIDE
    while at < end:
        slot, inner = at // 384, at % 384
        out[slot] = (inner, min(384 - inner, end - at))
        at += out[slot][1]
    return out


def product(weights, panels, i, row=0, height=8 * OWN):
    lhs = jnp.concatenate([weights[t, row : row + height] for t in range(8)], axis=1)
    blocks = []
    for slot, (inner, size) in slots(i).items():
        block = [panels[slot, t // 2, t % 2].reshape(4 * OWN, ROWS) for t in range(8)]
        blocks.append(jnp.concatenate(block, axis=1)[inner : inner + size])
    return lax.dot_general(
        lhs, jnp.concatenate(blocks, axis=0), NT, preferred_element_type=jnp.float32
    )


def finish(panels, weights, head, out_ref, tail, sems):
    z = lax.div(lax.axis_index("nuis"), 4)
    copies = []
    half = 4 * OWN

    def write(i, source, first, row=0, height=8 * OWN):
        at = first
        for slot, (inner, size) in slots(i).items():
            column = lax.rem(z + (DISTANCE[slot] + 8), 8) * 384 + inner
            copy = pltpu.make_async_copy(
                source.at[pl.ds(row, height), pl.ds(at, size)],
                out_ref.at[pl.ds(row, height), pl.ds(pl.multiple_of(column, 128), size)],
                sems.at[len(copies)],
            )
            copy.start()
            copies.append(copy)
            at += size

    for i in range(HEAD // WIDE):
        write(i, head, i * WIDE)
    waited = 0
    for i in range(HEAD // WIDE, 6):
        first = i * WIDE - HEAD
        for row in (0, half):
            tail[row : row + half, first : first + WIDE] = product(weights, panels, i, row, half)
            write(i, tail, first, row, half)
            copies[waited].wait()
            waited += 1
    for copy in copies[waited:]:
        copy.wait()


def kernel(
    deriv_in,
    ids_in,
    scale_in,
    coupling_in,
    second_in,
    third_in,
    offset_in,
    width_in,
    exp_in,
    panels,
    weights,
    out_ref,
    halo,
    expected,
    deriv_ref,
    ids_ref,
    scale_ref,
    coupling_ref,
    second_ref,
    third_ref,
    offset_ref,
    width_ref,
    exp_cols,
    exp_ref,
    operator_ref,
    gain_ref,
    in_sem,
    send_sem,
    recv_sem,
):
    b = lax.axis_index("bin")
    n = lax.axis_index("nuis")
    x, yh = lax.div(b, 2), lax.rem(b, 2)
    z, yl, c = lax.div(n, 4), lax.rem(lax.div(n, 2), 2), lax.rem(n, 2)
    y = yh * 2 + yl

    def device(dx=0, dy=0, dz=0, dc=0):
        nx = lax.rem(x + (dx + 4), 4) if dx else x
        ny = lax.rem(y + (dy + 4), 4) if dy else y
        nz = lax.rem(z + (dz + 8), 8) if dz else z
        nc = 1 - c if dc else c
        nyh, nyl = (lax.div(ny, 2), lax.rem(ny, 2)) if dy else (yh, yl)
        return (nx * 2 + nyh, nz * 4 + nyl * 2 + nc)

    inputs = [
        pltpu.make_async_copy(src, dst, in_sem.at[i])
        for i, (src, dst) in enumerate(
            (
                (second_in, second_ref),
                (third_in, third_ref),
                (offset_in, offset_ref),
                (width_in, width_ref),
                (scale_in, scale_ref),
                (ids_in, ids_ref),
                (coupling_in, coupling_ref),
                (exp_in, exp_cols),
                (deriv_in, deriv_ref),
            )
        )
    ]
    for copy in inputs:
        copy.start()

    partners = [dict(dx=dx, dy=dy) for dx in range(4) for dy in range(4) if dx or dy]
    partners += [dict(dz=dz) for dz in range(1, 8)] + [dict(dc=1)]
    barrier = pltpu.get_barrier_semaphore()
    for p in partners:
        pl.semaphore_signal(barrier, inc=1, device_id=device(**p), device_id_type=MESH)

    for copy in inputs[:6]:
        copy.wait()
    row = lax.broadcasted_iota(jnp.int32, (CELLS, CELLS), 0)
    col = lax.broadcasted_iota(jnp.int32, (CELLS, CELLS), 1)
    zero = jnp.zeros((CELLS, CELLS), jnp.float32)

    def chain(index, values):
        out = jnp.full((CELLS, CELLS), values[-1])
        for i in range(len(values) - 2, -1, -1):
            out = jnp.where(index == i, values[i], out)
        return out

    def banded(ref, i, j):
        out = zero
        for d in range(3):
            out = jnp.where(j - i == d - 1, chain(i, [ref[d, t] for t in range(4)]), out)
        return out

    r4, c4 = row & 7, col & 7
    offset = chain(r4, [offset_ref[t] for t in range(8)])
    width = chain(r4, [width_ref[t] for t in range(8)])
    inside = (c4 - r4 >= offset) & (c4 - r4 <= offset + width - 1)
    fourth = jnp.where(inside, 1.0 / width.astype(jnp.float32), zero)
    operator_ref[...] = (
        banded(second_ref, row >> 5, col >> 5)
        * (banded(third_ref, (row >> 3) & 3, (col >> 3) & 3) * fourth)
    )
    ids = ids_ref[...]
    gain = jnp.zeros((1, OWN), jnp.float32)
    for g in range(8):
        gain = jnp.where(ids == g, scale_ref[g], gain)
    gain_ref[...] = gain
    for copy in inputs[6:]:
        copy.wait()
    exp_ref[...] = exp_cols[...].T
    pl.semaphore_wait(barrier, len(partners))

    started = {}
    departed = {}
    arrived = set()

    def rows(count, wide=1):
        return weights.at[pl.ds(0, wide), pl.ds(0, count)]

    def send(event, departure, src, dst, target):
        copy = pltpu.make_async_remote_copy(
            src_ref=src,
            dst_ref=dst,
            send_sem=send_sem.at[DEPARTURES[departure]],
            recv_sem=recv_sem.at[EVENTS[event]],
            device_id=target,
            device_id_type=MESH,
        )
        copy.start()
        started[event] = copy
        departed[departure] = copy

    def empty(semaphore, like):
        pltpu.make_async_copy(like, like, semaphore).wait()

    def need(*events):
        for e in events:
            if e in arrived:
                continue
            arrived.add(e)
            semaphore = recv_sem.at[EVENTS[e]]
            if e == "exp":
                empty(semaphore, expected.at[pl.ds(0, 7)])
            elif e == "ap":
                empty(semaphore, rows(480))
            elif e[:2] in ("by", "cx"):
                empty(semaphore, rows(96 * GROUPS[int(e[2])][1]))
            elif e.startswith("coreN"):
                empty(semaphore, rows(768, GROUPS[int(e[5])][1]))
            elif e.startswith("coreF"):
                empty(semaphore, rows(256 * GROUPS[int(e[5])][1]))
            elif e[:2] in ("bf", "cf"):
                empty(semaphore, rows(128 * GROUPS[int(e[2])][1]))
            else:
                started[e].wait_recv()

    nb, pb = lax.rem(b + 1, 8), lax.rem(b + 7, 8)
    send("halo+", "halo+", deriv_ref.at[pl.ds(CELLS, CELLS)], halo.at[0], (nb, n))
    send("halo-", "halo-", deriv_ref.at[pl.ds(0, CELLS)], halo.at[1], (pb, n))
    for o in range(1, 8):
        peer = lax.rem(b + o, 8)
        send(
            "exp",
            "exp",
            exp_ref.at[pl.ds(pl.multiple_of(peer * 8, 8), 8)],
            expected.at[b],
            (peer, n),
        )
    expected[b] = exp_ref[pl.ds(pl.multiple_of(b * 8, 8), 8), :]
    first = deriv_ref[pl.ds(0, CELLS), :].astype(jnp.float32)
    second = deriv_ref[pl.ds(CELLS, CELLS), :].astype(jnp.float32)
    low0 = jnp.where(b == 0, 0.0, coupling_ref[0, 0])
    high1 = jnp.where(b == 7, 0.0, coupling_ref[1, 1])

    need("halo+", "halo-")
    below = halo[0].astype(jnp.float32)
    above = halo[1].astype(jnp.float32)
    mixed = (
        first + low0 * below + coupling_ref[1, 0] * second,
        second + coupling_ref[0, 1] * first + high1 * above,
    )
    for a in range(2):
        panel = lax.dot_general(
            operator_ref[...],
            mixed[a] * gain_ref[...],
            (((1,), (0,)), ((), ())),
            precision=lax.Precision.HIGHEST,
            preferred_element_type=jnp.float32,
        )
        panels[0, x, yh, yl, c, :, a * CELLS : (a + 1) * CELLS] = panel.T.astype(jnp.bfloat16)

    def own(slots, part, *place):
        lo, size = PART[part]
        return panels.at[(slots, *place, pl.ds(lo, size))]

    def along_z(s):
        for w, sign in (("+", 1), ("-", -1)):
            part = "BC" if s < 4 else ("B" if sign == 1 else "C")
            send(
                f"z{s}{w}",
                "z",
                own(0, part, x, yh, yl, c),
                own(SLOT[-sign * s], part, x, yh, yl, c),
                device(dz=sign * s),
            )

    def group(g):
        return pl.ds(*GROUPS[g])

    def group_here(g):
        if 1 <= g:
            need(f"z{g}+", f"z{g}-")

    def first_axis(g):
        group_here(g)
        mine_b = own(group(g), "B", x, yh, yl, c)
        mine_c = own(group(g), "C", x, yh, yl, c)
        for d in (1, 3, 2):
            send(f"by{g}", f"link{g}", mine_b, mine_b, device(dy=d))
            send(f"cx{g}", f"link{g}", mine_c, mine_c, device(dx=d))

    def second_axis(g):
        need(f"by{g}")
        line = own(group(g), "B", x, slice(None), slice(None), c)
        for w, sign in (("+", 1), ("-", -1)):
            send(f"bx{g}{w}", f"link{g}", line, line, device(dx=sign))
        need(f"cx{g}")
        line = own(group(g), "C", slice(None), yh, yl, c)
        for w, sign in (("+", 1), ("-", -1)):
            send(f"cy{g}{w}", f"link{g}", line, line, device(dy=sign))

    def far(g):
        for w, sign in (("+", 1), ("-", -1)):
            need(f"bx{g}{w}")
            line = own(group(g), "B", lax.rem(x + (4 - sign), 4), 0 if sign == 1 else 1, slice(None), c)
            send(f"bf{g}", f"link{g}", line, line, device(dx=sign))
        for w, sign in (("+", 1), ("-", -1)):
            need(f"cy{g}{w}")
            oy = lax.rem(y + (4 - sign), 4)
            line = own(group(g), "C", pl.ds(0 if sign == 1 else 2, 2), lax.div(oy, 2), lax.rem(oy, 2), c)
            send(f"cf{g}", f"link{g}", line, line, device(dy=sign))

    def plane_a():
        mine = own(0, "A", x, yh, yl, c)
        for dx in range(4):
            for dy in range(4):
                if dx or dy:
                    send("ap", "ap", mine, mine, device(dx=dx, dy=dy))

    def ring_a(s, h):
        for w, sign in (("+", 1), ("-", -1)):
            if f"az{s}{w}{h}" not in EVENTS:
                continue
            if s > 1:
                need(f"az{s - 1}{w}{h}")
            else:
                need("ap")
            place = (pl.ds(2 * h, 2), slice(None), slice(None), c)
            send(
                f"az{s}{w}{h}",
                "az",
                own(SLOT[-sign * (s - 1)], "A", *place),
                own(SLOT[-sign * s], "A", *place),
                device(dz=sign),
            )

    def own_a(g):
        if g == 0:
            need("ap")
        else:
            need(*[e for e in EVENTS if e.startswith(f"az{g}")])

    def share_near(g):
        for d in (0, 1, 3):
            line = own(group(g), "B", lax.rem(x + d, 4), slice(None), slice(None), c)
            send(f"coreN{g}", f"core{g}", line, line, device(dc=1))
            oy = lax.rem(y + d, 4)
            line = own(group(g), "C", slice(None), lax.div(oy, 2), lax.rem(oy, 2), c)
            send(f"coreN{g}", f"core{g}", line, line, device(dc=1))

    def share_far(g):
        need(f"bf{g}")
        line = own(group(g), "B", lax.rem(x + 2, 4), slice(None), slice(None), c)
        send(f"coreF{g}", f"core{g}", line, line, device(dc=1))
        need(f"cf{g}")
        oy = lax.rem(y + 2, 4)
        line = own(group(g), "C", slice(None), lax.div(oy, 2), lax.rem(oy, 2), c)
        send(f"coreF{g}", f"core{g}", line, line, device(dc=1))

    def share_a(g):
        own_a(g)
        block = own(group(g), "A", slice(None), slice(None), slice(None), c)
        send(f"coreA{g}", f"core{g}", block, block, device(dc=1))

    def weigh():
        need("exp")

        def body(t, _):
            inverse = 1.0 / expected[t] / (8.0 * ROWS)
            mine = panels[0, lax.div(t, 2), lax.rem(t, 2), yl, c].astype(jnp.float32)
            for k in range(8):
                weights[t, pl.ds(k * OWN, OWN), :] = (mine * inverse[k : k + 1, :]).astype(
                    jnp.bfloat16
                )
            return 0

        lax.fori_loop(0, 8, body, 0)

    def multiply(i):
        for slot in slots(i):
            need(*[f"core{p}{GROUP_OF[slot]}" for p in "ANF"])
        out_ref[:, i * WIDE : (i + 1) * WIDE] = product(weights, panels, i)

    along_z(1)
    first_axis(0)
    plane_a()
    along_z(2)
    along_z(3)
    along_z(4)
    first_axis(1)
    second_axis(0)
    first_axis(2)
    first_axis(3)
    ring_a(1, 0)
    ring_a(1, 1)
    first_axis(4)
    second_axis(1)
    far(0)
    share_near(0)
    share_a(0)
    second_axis(2)
    ring_a(2, 0)
    ring_a(2, 1)
    far(1)
    second_axis(3)
    share_near(1)
    share_far(0)
    share_a(1)
    weigh()
    ring_a(3, 0)
    far(2)
    second_axis(4)
    share_near(2)
    share_far(1)
    ring_a(3, 1)
    far(3)
    ring_a(4, 0)
    share_near(3)
    share_a(2)
    multiply(0)
    share_far(2)
    far(4)
    ring_a(4, 1)
    share_near(4)
    share_a(3)
    multiply(1)
    share_far(3)
    multiply(2)
    share_far(4)
    share_a(4)
    multiply(3)
    for g in range(5):
        need(*[f"core{p}{g}" for p in "ANF"])
    for d in DEPARTURES:
        semaphore = send_sem.at[DEPARTURES[d]]
        if d == "exp":
            empty(semaphore, expected.at[pl.ds(0, 7)])
        elif d == "ap":
            empty(semaphore, rows(480))
        elif d == "z":
            empty(semaphore, rows(448))
        elif d == "az":
            empty(semaphore, rows(512, 7))
        elif d.startswith("link"):
            empty(semaphore, rows(480, 2 * GROUPS[int(d[4])][1]))
        elif d.startswith("core"):
            empty(semaphore, panels.at[group(int(d[4])), :, :, :, 0])
        else:
            departed[d].wait_send()


def local(
    derivative,
    group_ids,
    group_scale,
    plane_coupling,
    band_second,
    band_third,
    band_offset,
    band_width,
    expected,
):
    flat = derivative.reshape(2 * CELLS, OWN)
    every = expected.transpose(1, 2, 3, 4, 0).reshape(ROWS, 64)
    hbm = pl.BlockSpec(memory_space=pltpu.HBM)
    vmem = pl.BlockSpec(memory_space=pltpu.VMEM)
    made = pl.pallas_call(
        kernel,
        out_shape=[
            pltpu.VMEM((8, 4, 2, 2, 2, OWN, ROWS), jnp.bfloat16),
            pltpu.VMEM((8, 8 * OWN, ROWS), jnp.bfloat16),
            pltpu.VMEM((8 * OWN, HEAD), jnp.float32),
        ],
        in_specs=[hbm] * 9,
        out_specs=[vmem] * 3,
        scratch_shapes=[
            pltpu.VMEM((2, CELLS, OWN), jnp.bfloat16),
            pltpu.VMEM((8, 8, ROWS), jnp.float32),
            pltpu.VMEM((2 * CELLS, OWN), jnp.bfloat16),
            pltpu.VMEM((1, OWN), jnp.int32),
            pltpu.SMEM((8,), jnp.float32),
            pltpu.SMEM((2, 2), jnp.float32),
            pltpu.SMEM((3, 4), jnp.float32),
            pltpu.SMEM((3, 4), jnp.float32),
            pltpu.SMEM((8,), jnp.int32),
            pltpu.SMEM((8,), jnp.int32),
            pltpu.VMEM((ROWS, 64), jnp.float32),
            pltpu.VMEM((64, ROWS), jnp.float32),
            pltpu.VMEM((CELLS, CELLS), jnp.float32),
            pltpu.VMEM((1, OWN), jnp.float32),
            pltpu.SemaphoreType.DMA((9,)),
            pltpu.SemaphoreType.DMA((len(DEPARTURES),)),
            pltpu.SemaphoreType.DMA((len(EVENTS),)),
        ],
        compiler_params=pltpu.CompilerParams(
            collective_id=0, has_side_effects=True, vmem_limit_bytes=16 * 1024 * 1024
        ),
        cost_estimate=pl.CostEstimate(
            flops=2 * 768 * 2048 * HEAD, bytes_accessed=10_000_000, transcendentals=0
        ),
        name="fisher",
    )(
        *[
            pltpu.with_memory_space_constraint(a, pltpu.HBM)
            for a in (
                flat,
                group_ids.reshape(1, OWN),
                group_scale,
                plane_coupling,
                band_second,
                band_third,
                band_offset,
                band_width,
                every,
            )
        ]
    )
    out = pl.pallas_call(
        finish,
        out_shape=jax.ShapeDtypeStruct((8 * OWN, 3072), jnp.float32),
        in_specs=[vmem] * 3,
        out_specs=hbm,
        scratch_shapes=[
            pltpu.VMEM((8 * OWN, 3072 - HEAD), jnp.float32),
            pltpu.SemaphoreType.DMA((24,)),
        ],
        compiler_params=pltpu.CompilerParams(vmem_limit_bytes=16 * 1024 * 1024),
        cost_estimate=pl.CostEstimate(
            flops=2 * 768 * 2048 * (3072 - HEAD), bytes_accessed=10_000_000, transcendentals=0
        ),
        name="finish",
    )(*[pltpu.with_memory_space_constraint(a, pltpu.VMEM) for a in made])
    return out.reshape(8, OWN, 3072)


def solution(mesh):
    placed = (
        P("bin", None, None, None, "nuis"),
        P("nuis"),
        P(),
        P(None, "bin"),
        P(),
        P(),
        P(),
        P(),
        P(None, "bin", None, None, None),
    )
    return jax.shard_map(
        local, mesh=mesh, in_specs=placed, out_specs=P("bin", "nuis", None), check_vma=False
    )
```

```python
import functools

import jax
import jax.numpy as jnp
from jax import lax
from jax.experimental import pallas as pl
from jax.experimental.pallas import tpu as pltpu
from jax.sharding import PartitionSpec as P

MESH = pl.DeviceIdType.MESH
NT = (((1,), (1,)), ((), ()))
CELLS = 128
OWN = 96
ROWS = 256
SLOT = {0: 0, 1: 1, -1: 2, 2: 3, -2: 4, 3: 5, -3: 6, 4: 7, -4: 7}
DISTANCE = (0, 1, -1, 2, -2, 3, -3, 4)
GROUPS = ((0, 1), (1, 2), (3, 2), (5, 2), (7, 1))
GROUP_OF = (0, 1, 1, 2, 2, 3, 3, 4)
WIDE = 512
PART = {"A": (0, 32),  "B": (32, 32), "C": (64, 32), "B0": (32, 16), "B1": (48, 16), "C0": (64, 16), "C1": (80, 16), "BC": (32, 64)}


HEAD = 2048


def ring_signs(s, h):
    return (1, -1) if s < 4 else ((1,), (-1,))[h]


def events():
    out = {"halo+": 0, "halo-": 0, "exp": 0, "ap": 480}
    for s in range(1, 5):
        out[f"z{s}"] = 128 if s < 4 else 64
        for h in range(2):
            for sign in ring_signs(s, h):
                out[f"az{s}{h}{sign}"] = 256
    for g, (_, n) in enumerate(GROUPS):
        if g in RELAYED:
            out[f"near{g}"], out[f"relay{g}"] = 128 * n, 64 * n
        else:
            out[f"first{g}"] = 192 * n
        for sign in (1, -1):
            out[f"bx{g}{sign}"] = out[f"cy{g}{sign}"] = 128 * n
        out[f"far{g}"], out[f"core{g}"] = 256 * n, 1536 * n
    return out


RELAYED = (3, 4)
COUNTS = events()
EVENTS = {n: i for i, n in enumerate(COUNTS)}
DEPARTURES = {n: i for i, n in enumerate(("halo+", "halo-", "exp", "ap", "z", "az", "link", "core"))}


def slots(i):
    out, at, end = {}, i * WIDE, (i + 1) * WIDE
    while at < end:
        slot, inner = at // 384, at % 384
        out[slot] = (inner, min(384 - inner, end - at))
        at += out[slot][1]
    return out


def product(weights, panels, i, row=0, height=8 * OWN):
    lhs = jnp.concatenate([weights[t, row : row + height] for t in range(8)], axis=1)
    blocks = []
    for slot, (inner, size) in slots(i).items():
        block = [panels[slot, t // 2, t % 2].reshape(4 * OWN, ROWS) for t in range(8)]
        blocks.append(jnp.concatenate(block, axis=1)[inner : inner + size])
    return lax.dot_general(
        lhs, jnp.concatenate(blocks, axis=0), NT, preferred_element_type=jnp.float32
    )


def finish(panels, weights, head, out_ref, tail, sems):
    z = lax.div(lax.axis_index("nuis"), 4)
    half = 4 * OWN

    def write(i, source, first, semaphore, row=0, height=8 * OWN):
        at = first
        for slot, (inner, size) in slots(i).items():
            column = lax.rem(z + (DISTANCE[slot] + 8), 8) * 384 + inner
            pltpu.make_async_copy(
                source.at[pl.ds(row, height), pl.ds(at, size)],
                out_ref.at[pl.ds(row, height), pl.ds(pl.multiple_of(column, 128), size)],
                semaphore,
            ).start()
            at += size

    def written(semaphore, height=8 * OWN):
        block = head.at[pl.ds(0, height), pl.ds(0, WIDE)]
        pltpu.make_async_copy(block, block, semaphore).wait()

    early = HEAD // WIDE
    for i in range(early):
        write(i, head, i * WIDE, sems.at[i])
    step = 0
    for i in range(early, 6):
        first = i * WIDE - HEAD
        for row in (0, half):
            tail[row : row + half, first : first + WIDE] = product(weights, panels, i, row, half)
            write(i, tail, first, sems.at[early + step], row, half)
            written(sems.at[step])
            step += 1
    for i in range(step):
        written(sems.at[early + i], half)


def kernel(
    deriv_in,
    ids_in,
    scale_in,
    coupling_in,
    second_in,
    third_in,
    offset_in,
    width_in,
    exp_in,
    panels,
    weights,
    out_ref,
    halo,
    expected,
    deriv_ref,
    ids_ref,
    scale_ref,
    coupling_ref,
    second_ref,
    third_ref,
    offset_ref,
    width_ref,
    exp_cols,
    exp_ref,
    operator_ref,
    gain_ref,
    in_sem,
    send_sem,
    recv_sem,
):
    b = lax.axis_index("bin")
    n = lax.axis_index("nuis")
    x, yh = lax.div(b, 2), lax.rem(b, 2)
    z, yl, c = lax.div(n, 4), lax.rem(lax.div(n, 2), 2), lax.rem(n, 2)
    y = yh * 2 + yl

    def device(dx=0, dy=0, dz=0, dc=0):
        nx = lax.rem(x + (dx + 4), 4) if dx else x
        ny = lax.rem(y + (dy + 4), 4) if dy else y
        nz = lax.rem(z + (dz + 8), 8) if dz else z
        nc = 1 - c if dc else c
        nyh, nyl = (lax.div(ny, 2), lax.rem(ny, 2)) if dy else (yh, yl)
        return (nx * 2 + nyh, nz * 4 + nyl * 2 + nc)

    inputs = [
        pltpu.make_async_copy(src, dst, in_sem.at[i])
        for i, (src, dst) in enumerate(
            (
                (second_in, second_ref),
                (third_in, third_ref),
                (offset_in, offset_ref),
                (width_in, width_ref),
                (scale_in, scale_ref),
                (ids_in, ids_ref),
                (coupling_in, coupling_ref),
                (exp_in, exp_cols),
                (deriv_in, deriv_ref),
            )
        )
    ]
    for copy in inputs:
        copy.start()

    partners = [dict(dx=dx, dy=dy) for dx in range(4) for dy in range(4) if dx or dy]
    partners += [dict(dz=dz) for dz in range(1, 8)] + [dict(dc=1)]
    barrier = pltpu.get_barrier_semaphore()
    for p in partners:
        pl.semaphore_signal(barrier, inc=1, device_id=device(**p), device_id_type=MESH)

    for copy in inputs[:6]:
        copy.wait()
    row = lax.broadcasted_iota(jnp.int32, (CELLS, CELLS), 0)
    col = lax.broadcasted_iota(jnp.int32, (CELLS, CELLS), 1)
    zero = jnp.zeros((CELLS, CELLS), jnp.float32)

    def chain(index, values):
        out = jnp.full((CELLS, CELLS), values[-1])
        for i in range(len(values) - 2, -1, -1):
            out = jnp.where(index == i, values[i], out)
        return out

    def banded(ref, i, j):
        out = zero
        for d in range(3):
            out = jnp.where(j - i == d - 1, chain(i, [ref[d, t] for t in range(4)]), out)
        return out

    r4, c4 = row & 7, col & 7
    offset = chain(r4, [offset_ref[t] for t in range(8)])
    width = chain(r4, [width_ref[t] for t in range(8)])
    inside = (c4 - r4 >= offset) & (c4 - r4 <= offset + width - 1)
    fourth = jnp.where(inside, 1.0 / width.astype(jnp.float32), zero)
    operator_ref[...] = (
        banded(second_ref, row >> 5, col >> 5)
        * (banded(third_ref, (row >> 3) & 3, (col >> 3) & 3) * fourth)
    )
    ids = ids_ref[...]
    gain = jnp.zeros((1, OWN), jnp.float32)
    for g in range(8):
        gain = jnp.where(ids == g, scale_ref[g], gain)
    gain_ref[...] = gain
    for copy in inputs[6:]:
        copy.wait()
    exp_ref[...] = exp_cols[...].T
    pl.semaphore_wait(barrier, len(partners))

    started = {}
    departed = {}
    arrived = set()

    def rows(count):
        wide = 1
        while count // wide > 8 * OWN:
            wide *= 2
        return weights.at[pl.ds(0, wide), pl.ds(0, count // wide)]

    def send(event, departure, src, dst, target):
        copy = pltpu.make_async_remote_copy(
            src_ref=src,
            dst_ref=dst,
            send_sem=send_sem.at[DEPARTURES[departure]],
            recv_sem=recv_sem.at[EVENTS[event]],
            device_id=target,
            device_id_type=MESH,
        )
        copy.start()
        started[event] = copy
        departed[departure] = copy

    def empty(semaphore, like):
        pltpu.make_async_copy(like, like, semaphore).wait()

    def need(*events):
        for e in events:
            if e in arrived:
                continue
            arrived.add(e)
            semaphore = recv_sem.at[EVENTS[e]]
            if e == "exp":
                empty(semaphore, expected.at[pl.ds(0, 7)])
            elif COUNTS[e]:
                empty(semaphore, rows(COUNTS[e]))
            else:
                started[e].wait_recv()

    nb, pb = lax.rem(b + 1, 8), lax.rem(b + 7, 8)
    send("halo+", "halo+", deriv_ref.at[pl.ds(CELLS, CELLS)], halo.at[0], (nb, n))
    send("halo-", "halo-", deriv_ref.at[pl.ds(0, CELLS)], halo.at[1], (pb, n))
    for o in range(1, 8):
        peer = lax.rem(b + o, 8)
        send(
            "exp",
            "exp",
            exp_ref.at[pl.ds(pl.multiple_of(peer * 8, 8), 8)],
            expected.at[b],
            (peer, n),
        )
    expected[b] = exp_ref[pl.ds(pl.multiple_of(b * 8, 8), 8), :]
    first = deriv_ref[pl.ds(0, CELLS), :].astype(jnp.float32)
    second = deriv_ref[pl.ds(CELLS, CELLS), :].astype(jnp.float32)
    low0 = jnp.where(b == 0, 0.0, coupling_ref[0, 0])
    high1 = jnp.where(b == 7, 0.0, coupling_ref[1, 1])

    need("halo+", "halo-")
    below = halo[0].astype(jnp.float32)
    above = halo[1].astype(jnp.float32)
    mixed = (
        first + low0 * below + coupling_ref[1, 0] * second,
        second + coupling_ref[0, 1] * first + high1 * above,
    )
    for a in range(2):
        panel = lax.dot_general(
            operator_ref[...],
            mixed[a] * gain_ref[...],
            (((1,), (0,)), ((), ())),
            precision=lax.Precision.HIGHEST,
            preferred_element_type=jnp.float32,
        )
        panels[0, x, yh, yl, c, :, a * CELLS : (a + 1) * CELLS] = panel.T.astype(jnp.bfloat16)

    def own(slots, part, *place):
        lo, size = PART[part]
        return panels.at[(slots, *place, pl.ds(lo, size))]

    def along_z(s):
        for w, sign in (("+", 1), ("-", -1)):
            part = "BC" if s < 4 else ("B" if sign == 1 else "C")
            send(
                f"z{s}",
                "z",
                own(0, part, x, yh, yl, c),
                own(SLOT[-sign * s], part, x, yh, yl, c),
                device(dz=sign * s),
            )

    def group(g):
        return pl.ds(*GROUPS[g])

    def first_axis(g):
        if g:
            need(f"z{g}")
        mine_b = own(group(g), "B", x, yh, yl, c)
        mine_c = own(group(g), "C", x, yh, yl, c)
        event = f"near{g}" if g in RELAYED else f"first{g}"
        for d in (1, 3) if g in RELAYED else (1, 3, 2):
            send(event, "link", mine_b, mine_b, device(dy=d))
            send(event, "link", mine_c, mine_c, device(dx=d))

    def relay(g):
        need(f"near{g}")
        for half, sign in (("0", 1), ("1", -1)):
            oy = lax.rem(y + (4 - sign), 4)
            piece = own(group(g), "B" + half, x, lax.div(oy, 2), lax.rem(oy, 2), c)
            send(f"relay{g}", "link", piece, piece, device(dy=sign))
            piece = own(group(g), "C" + half, lax.rem(x + (4 - sign), 4), yh, yl, c)
            send(f"relay{g}", "link", piece, piece, device(dx=sign))

    def second_axis(g):
        if g in RELAYED:
            need(f"near{g}", f"relay{g}")
        else:
            need(f"first{g}")
        row = own(group(g), "B", x, slice(None), slice(None), c)
        column = own(group(g), "C", slice(None), yh, yl, c)
        for sign in (1, -1):
            send(f"bx{g}{sign}", "link", row, row, device(dx=sign))
            send(f"cy{g}{sign}", "link", column, column, device(dy=sign))

    def far(g):
        for i, sign in enumerate((1, -1)):
            need(f"bx{g}{sign}")
            line = own(group(g), "B", lax.rem(x + (4 - sign), 4), i, slice(None), c)
            send(f"far{g}", "link", line, line, device(dx=sign))
            need(f"cy{g}{sign}")
            oy = lax.rem(y + (4 - sign), 4)
            line = own(group(g), "C", pl.ds(2 * i, 2), lax.div(oy, 2), lax.rem(oy, 2), c)
            send(f"far{g}", "link", line, line, device(dy=sign))

    def plane_a():
        mine = own(0, "A", x, yh, yl, c)
        for dx in range(4):
            for dy in range(4):
                if dx or dy:
                    send("ap", "ap", mine, mine, device(dx=dx, dy=dy))

    def ring_a(s, h):
        place = (pl.ds(2 * h, 2), slice(None), slice(None), c)
        for sign in ring_signs(s, h):
            need("ap" if s == 1 else f"az{s - 1}{h}{sign}")
            send(
                f"az{s}{h}{sign}",
                "az",
                own(SLOT[-sign * (s - 1)], "A", *place),
                own(SLOT[-sign * s], "A", *place),
                device(dz=sign),
            )

    def own_a(g):
        if g == 0:
            need("ap")
        else:
            need(*[f"az{g}{h}{sign}" for h in range(2) for sign in ring_signs(g, h)])

    def share_near(g):
        for d in (0, 1, 3):
            line = own(group(g), "B", lax.rem(x + d, 4), slice(None), slice(None), c)
            send(f"core{g}", "core", line, line, device(dc=1))
            oy = lax.rem(y + d, 4)
            line = own(group(g), "C", slice(None), lax.div(oy, 2), lax.rem(oy, 2), c)
            send(f"core{g}", "core", line, line, device(dc=1))

    def share_far(g):
        need(f"far{g}")
        line = own(group(g), "B", lax.rem(x + 2, 4), slice(None), slice(None), c)
        send(f"core{g}", "core", line, line, device(dc=1))
        oy = lax.rem(y + 2, 4)
        line = own(group(g), "C", slice(None), lax.div(oy, 2), lax.rem(oy, 2), c)
        send(f"core{g}", "core", line, line, device(dc=1))

    def share_a(g):
        own_a(g)
        block = own(group(g), "A", slice(None), slice(None), slice(None), c)
        send(f"core{g}", "core", block, block, device(dc=1))

    def weigh():
        need("exp")

        def body(t, _):
            inverse = 1.0 / expected[t] / (8.0 * ROWS)
            mine = panels[0, lax.div(t, 2), lax.rem(t, 2), yl, c].astype(jnp.float32)
            for k in range(8):
                weights[t, pl.ds(k * OWN, OWN), :] = (mine * inverse[k : k + 1, :]).astype(
                    jnp.bfloat16
                )
            return 0

        lax.fori_loop(0, 8, body, 0)

    def multiply(i):
        for slot in slots(i):
            need(f"core{GROUP_OF[slot]}")
        out_ref[:, i * WIDE : (i + 1) * WIDE] = product(weights, panels, i)

    along_z(1)
    first_axis(0)
    plane_a()
    along_z(2)
    along_z(3)
    along_z(4)
    first_axis(1)
    second_axis(0)
    first_axis(2)
    first_axis(3)
    ring_a(1, 0)
    ring_a(1, 1)
    first_axis(4)
    second_axis(1)
    far(0)
    share_near(0)
    share_a(0)
    relay(3)
    second_axis(2)
    relay(4)
    ring_a(2, 0)
    ring_a(2, 1)
    far(1)
    second_axis(3)
    share_near(1)
    share_far(0)
    share_a(1)
    weigh()
    ring_a(3, 0)
    far(2)
    second_axis(4)
    share_near(2)
    share_far(1)
    ring_a(3, 1)
    far(3)
    ring_a(4, 0)
    share_near(3)
    share_a(2)
    multiply(0)
    share_far(2)
    far(4)
    ring_a(4, 1)
    share_near(4)
    share_a(3)
    multiply(1)
    share_far(3)
    multiply(2)
    share_far(4)
    share_a(4)
    multiply(3)
    for g in range(5):
        need(f"core{g}")
    for d, i in DEPARTURES.items():
        semaphore = send_sem.at[i]
        if d == "exp":
            empty(semaphore, expected.at[pl.ds(0, 7)])
        elif d == "ap":
            empty(semaphore, rows(480))
        elif d == "z":
            empty(semaphore, rows(448))
        elif d == "az":
            empty(semaphore, rows(3584))
        elif d == "link":
            empty(semaphore, panels.at[pl.ds(0, 5), :, :, :, 0])
        elif d == "core":
            empty(semaphore, panels.at[pl.ds(0, 4)])
        else:
            departed[d].wait_send()


def local(
    derivative,
    group_ids,
    group_scale,
    plane_coupling,
    band_second,
    band_third,
    band_offset,
    band_width,
    expected,
):
    flat = derivative.reshape(2 * CELLS, OWN)
    every = expected.transpose(1, 2, 3, 4, 0).reshape(ROWS, 64)
    hbm = pl.BlockSpec(memory_space=pltpu.HBM)
    vmem = pl.BlockSpec(memory_space=pltpu.VMEM)
    made = pl.pallas_call(
        kernel,
        out_shape=[
            pltpu.VMEM((8, 4, 2, 2, 2, OWN, ROWS), jnp.bfloat16),
            pltpu.VMEM((8, 8 * OWN, ROWS), jnp.bfloat16),
            pltpu.VMEM((8 * OWN, HEAD), jnp.float32),
        ],
        in_specs=[hbm] * 9,
        out_specs=[vmem] * 3,
        scratch_shapes=[
            pltpu.VMEM((2, CELLS, OWN), jnp.bfloat16),
            pltpu.VMEM((8, 8, ROWS), jnp.float32),
            pltpu.VMEM((2 * CELLS, OWN), jnp.bfloat16),
            pltpu.VMEM((1, OWN), jnp.int32),
            pltpu.SMEM((8,), jnp.float32),
            pltpu.SMEM((2, 2), jnp.float32),
            pltpu.SMEM((3, 4), jnp.float32),
            pltpu.SMEM((3, 4), jnp.float32),
            pltpu.SMEM((8,), jnp.int32),
            pltpu.SMEM((8,), jnp.int32),
            pltpu.VMEM((ROWS, 64), jnp.float32),
            pltpu.VMEM((64, ROWS), jnp.float32),
            pltpu.VMEM((CELLS, CELLS), jnp.float32),
            pltpu.VMEM((1, OWN), jnp.float32),
            pltpu.SemaphoreType.DMA((9,)),
            pltpu.SemaphoreType.DMA((len(DEPARTURES),)),
            pltpu.SemaphoreType.DMA((len(EVENTS),)),
        ],
        compiler_params=pltpu.CompilerParams(
            collective_id=0, has_side_effects=True, vmem_limit_bytes=16 * 1024 * 1024
        ),
        cost_estimate=pl.CostEstimate(
            flops=2 * 768 * 2048 * HEAD, bytes_accessed=10_000_000, transcendentals=0
        ),
        name="fisher",
    )(
        *[
            pltpu.with_memory_space_constraint(a, pltpu.HBM)
            for a in (
                flat,
                group_ids.reshape(1, OWN),
                group_scale,
                plane_coupling,
                band_second,
                band_third,
                band_offset,
                band_width,
                every,
            )
        ]
    )
    out = pl.pallas_call(
        finish,
        out_shape=jax.ShapeDtypeStruct((8 * OWN, 3072), jnp.float32),
        in_specs=[vmem] * 3,
        out_specs=hbm,
        scratch_shapes=[
            pltpu.VMEM((8 * OWN, 3072 - HEAD), jnp.float32),
            pltpu.SemaphoreType.DMA((8,)),
        ],
        compiler_params=pltpu.CompilerParams(vmem_limit_bytes=16 * 1024 * 1024),
        cost_estimate=pl.CostEstimate(
            flops=2 * 768 * 2048 * (3072 - HEAD), bytes_accessed=10_000_000, transcendentals=0
        ),
        name="finish",
    )(*[pltpu.with_memory_space_constraint(a, pltpu.VMEM) for a in made])
    return out.reshape(8, OWN, 3072)


def solution(mesh):
    placed = (
        P("bin", None, None, None, "nuis"),
        P("nuis"),
        P(),
        P(None, "bin"),
        P(),
        P(),
        P(),
        P(),
        P(None, "bin", None, None, None),
    )
    return jax.shard_map(
        local, mesh=mesh, in_specs=placed, out_specs=P("bin", "nuis", None), check_vma=False
    )
```

```python
import functools

import jax
import jax.numpy as jnp
from jax import lax
from jax.experimental import pallas as pl
from jax.experimental.pallas import tpu as pltpu
from jax.sharding import PartitionSpec as P

MESH = pl.DeviceIdType.MESH
NT = (((1,), (1,)), ((), ()))
CELLS = 128
OWN = 96
ROWS = 256
SLOT = {0: 0, 1: 1, -1: 2, 2: 3, -2: 4, 3: 5, -3: 6, 4: 7, -4: 7}
DISTANCE = (0, 1, -1, 2, -2, 3, -3, 4)
GROUPS = ((0, 1), (1, 2), (3, 2), (5, 2), (7, 1))
GROUP_OF = (0, 1, 1, 2, 2, 3, 3, 4)
WIDE = 512
PART = {"A": (0, 32),  "B": (32, 32), "C": (64, 32), "B0": (32, 16), "B1": (48, 16), "C0": (64, 16), "C1": (80, 16), "BC": (32, 64)}


HEAD = 2048


def ring_signs(s, h):
    return (1, -1) if s < 4 else ((1,), (-1,))[h]


def events():
    out = {"halo+": 0, "halo-": 0, "exp": 0, "ap": 480}
    for s in range(1, 5):
        out[f"z{s}"] = 128 if s < 4 else 64
        for h in range(2):
            for sign in ring_signs(s, h):
                out[f"az{s}{h}{sign}"] = 256
    for g, (_, n) in enumerate(GROUPS):
        if g in RELAYED:
            out[f"near{g}"], out[f"relay{g}"] = 128 * n, 64 * n
        else:
            out[f"first{g}"] = 192 * n
        for sign in (1, -1):
            out[f"bx{g}{sign}"] = out[f"cy{g}{sign}"] = 128 * n
        out[f"far{g}"], out[f"core{g}"] = 256 * n, 1536 * n
    return out


RELAYED = (3, 4)
COUNTS = events()
EVENTS = {n: i for i, n in enumerate(COUNTS)}
DEPARTURES = {n: i for i, n in enumerate(("halo+", "halo-", "exp", "ap", "z", "az", "link", "core"))}


def slots(i):
    out, at, end = {}, i * WIDE, (i + 1) * WIDE
    while at < end:
        slot, inner = at // 384, at % 384
        out[slot] = (inner, min(384 - inner, end - at))
        at += out[slot][1]
    return out


def product(weights, panels, i, row=0, height=8 * OWN):
    lhs = jnp.concatenate([weights[t, row : row + height] for t in range(8)], axis=1)
    blocks = []
    for slot, (inner, size) in slots(i).items():
        block = [panels[slot, t // 2, t % 2].reshape(4 * OWN, ROWS) for t in range(8)]
        blocks.append(jnp.concatenate(block, axis=1)[inner : inner + size])
    return lax.dot_general(
        lhs, jnp.concatenate(blocks, axis=0), NT, preferred_element_type=jnp.float32
    )


def finish(panels, weights, head, out_ref, tail, sems):
    z = lax.div(lax.axis_index("nuis"), 4)
    half = 4 * OWN

    def write(i, source, first, semaphore, row=0, height=8 * OWN):
        at = first
        for slot, (inner, size) in slots(i).items():
            column = lax.rem(z + (DISTANCE[slot] + 8), 8) * 384 + inner
            pltpu.make_async_copy(
                source.at[pl.ds(row, height), pl.ds(at, size)],
                out_ref.at[pl.ds(row, height), pl.ds(pl.multiple_of(column, 128), size)],
                semaphore,
            ).start()
            at += size

    def written(semaphore, height=8 * OWN):
        block = head.at[pl.ds(0, height), pl.ds(0, WIDE)]
        pltpu.make_async_copy(block, block, semaphore).wait()

    early = HEAD // WIDE
    for i in range(early):
        write(i, head, i * WIDE, sems.at[i])
    step = 0
    for i in range(early, 6):
        first = i * WIDE - HEAD
        for row in (0, half):
            tail[row : row + half, first : first + WIDE] = product(weights, panels, i, row, half)
            write(i, tail, first, sems.at[early + step], row, half)
            written(sems.at[step])
            step += 1
    for i in range(step):
        written(sems.at[early + i], half)


def kernel(
    deriv_in,
    ids_in,
    scale_in,
    coupling_in,
    second_in,
    third_in,
    offset_in,
    width_in,
    exp_in,
    panels,
    weights,
    out_ref,
    halo,
    expected,
    deriv_ref,
    ids_ref,
    scale_ref,
    coupling_ref,
    second_ref,
    third_ref,
    offset_ref,
    width_ref,
    exp_cols,
    exp_ref,
    operator_ref,
    gain_ref,
    in_sem,
    send_sem,
    recv_sem,
):
    b = lax.axis_index("bin")
    n = lax.axis_index("nuis")
    x, yh = lax.div(b, 2), lax.rem(b, 2)
    z, yl, c = lax.div(n, 4), lax.rem(lax.div(n, 2), 2), lax.rem(n, 2)
    y = yh * 2 + yl

    def device(dx=0, dy=0, dz=0, dc=0):
        nx = lax.rem(x + (dx + 4), 4) if dx else x
        ny = lax.rem(y + (dy + 4), 4) if dy else y
        nz = lax.rem(z + (dz + 8), 8) if dz else z
        nc = 1 - c if dc else c
        nyh, nyl = (lax.div(ny, 2), lax.rem(ny, 2)) if dy else (yh, yl)
        return (nx * 2 + nyh, nz * 4 + nyl * 2 + nc)

    inputs = [
        pltpu.make_async_copy(src, dst, in_sem.at[i])
        for i, (src, dst) in enumerate(
            (
                (second_in, second_ref),
                (third_in, third_ref),
                (offset_in, offset_ref),
                (width_in, width_ref),
                (scale_in, scale_ref),
                (ids_in, ids_ref),
                (coupling_in, coupling_ref),
                (exp_in, exp_cols),
                (deriv_in, deriv_ref),
            )
        )
    ]
    for copy in inputs:
        copy.start()

    partners = [dict(dx=dx, dy=dy) for dx in range(4) for dy in range(4) if dx or dy]
    partners += [dict(dz=dz) for dz in range(1, 8)] + [dict(dc=1)]
    barrier = pltpu.get_barrier_semaphore()
    for p in partners:
        pl.semaphore_signal(barrier, inc=1, device_id=device(**p), device_id_type=MESH)

    inputs[8].wait()
    pl.semaphore_wait(barrier, len(partners))

    started = {}
    departed = {}
    arrived = set()

    def rows(count):
        wide = 1
        while count // wide > 8 * OWN:
            wide *= 2
        return weights.at[pl.ds(0, wide), pl.ds(0, count // wide)]

    def send(event, departure, src, dst, target):
        copy = pltpu.make_async_remote_copy(
            src_ref=src,
            dst_ref=dst,
            send_sem=send_sem.at[DEPARTURES[departure]],
            recv_sem=recv_sem.at[EVENTS[event]],
            device_id=target,
            device_id_type=MESH,
        )
        copy.start()
        started[event] = copy
        departed[departure] = copy

    def empty(semaphore, like):
        pltpu.make_async_copy(like, like, semaphore).wait()

    def need(*events):
        for e in events:
            if e in arrived:
                continue
            arrived.add(e)
            semaphore = recv_sem.at[EVENTS[e]]
            if e == "exp":
                empty(semaphore, expected.at[pl.ds(0, 7)])
            elif COUNTS[e]:
                empty(semaphore, rows(COUNTS[e]))
            else:
                started[e].wait_recv()

    nb, pb = lax.rem(b + 1, 8), lax.rem(b + 7, 8)
    send("halo+", "halo+", deriv_ref.at[pl.ds(CELLS, CELLS)], halo.at[0], (nb, n))
    send("halo-", "halo-", deriv_ref.at[pl.ds(0, CELLS)], halo.at[1], (pb, n))
    for copy in inputs[:8]:
        copy.wait()
    exp_ref[...] = exp_cols[...].T
    for o in range(1, 8):
        peer = lax.rem(b + o, 8)
        send(
            "exp",
            "exp",
            exp_ref.at[pl.ds(pl.multiple_of(peer * 8, 8), 8)],
            expected.at[b],
            (peer, n),
        )
    expected[b] = exp_ref[pl.ds(pl.multiple_of(b * 8, 8), 8), :]
    row = lax.broadcasted_iota(jnp.int32, (CELLS, CELLS), 0)
    col = lax.broadcasted_iota(jnp.int32, (CELLS, CELLS), 1)
    zero = jnp.zeros((CELLS, CELLS), jnp.float32)

    def chain(index, values):
        out = jnp.full((CELLS, CELLS), values[-1])
        for i in range(len(values) - 2, -1, -1):
            out = jnp.where(index == i, values[i], out)
        return out

    def banded(ref, i, j):
        out = zero
        for d in range(3):
            out = jnp.where(j - i == d - 1, chain(i, [ref[d, t] for t in range(4)]), out)
        return out

    r4, c4 = row & 7, col & 7
    offset = chain(r4, [offset_ref[t] for t in range(8)])
    width = chain(r4, [width_ref[t] for t in range(8)])
    inside = (c4 - r4 >= offset) & (c4 - r4 <= offset + width - 1)
    fourth = jnp.where(inside, 1.0 / width.astype(jnp.float32), zero)
    operator_ref[...] = (
        banded(second_ref, row >> 5, col >> 5)
        * (banded(third_ref, (row >> 3) & 3, (col >> 3) & 3) * fourth)
    )
    ids = ids_ref[...]
    gain = jnp.zeros((1, OWN), jnp.float32)
    for g in range(8):
        gain = jnp.where(ids == g, scale_ref[g], gain)
    gain_ref[...] = gain
    first = deriv_ref[pl.ds(0, CELLS), :].astype(jnp.float32)
    second = deriv_ref[pl.ds(CELLS, CELLS), :].astype(jnp.float32)
    low0 = jnp.where(b == 0, 0.0, coupling_ref[0, 0])
    high1 = jnp.where(b == 7, 0.0, coupling_ref[1, 1])

    need("halo+", "halo-")
    below = halo[0].astype(jnp.float32)
    above = halo[1].astype(jnp.float32)
    mixed = (
        first + low0 * below + coupling_ref[1, 0] * second,
        second + coupling_ref[0, 1] * first + high1 * above,
    )
    for a in range(2):
        panel = lax.dot_general(
            operator_ref[...],
            mixed[a] * gain_ref[...],
            (((1,), (0,)), ((), ())),
            precision=lax.Precision.HIGHEST,
            preferred_element_type=jnp.float32,
        )
        panels[0, x, yh, yl, c, :, a * CELLS : (a + 1) * CELLS] = panel.T.astype(jnp.bfloat16)

    def own(slots, part, *place):
        lo, size = PART[part]
        return panels.at[(slots, *place, pl.ds(lo, size))]

    def along_z(s):
        for w, sign in (("+", 1), ("-", -1)):
            part = "BC" if s < 4 else ("B" if sign == 1 else "C")
            send(
                f"z{s}",
                "z",
                own(0, part, x, yh, yl, c),
                own(SLOT[-sign * s], part, x, yh, yl, c),
                device(dz=sign * s),
            )

    def group(g):
        return pl.ds(*GROUPS[g])

    def first_axis(g):
        if g:
            need(f"z{g}")
        mine_b = own(group(g), "B", x, yh, yl, c)
        mine_c = own(group(g), "C", x, yh, yl, c)
        event = f"near{g}" if g in RELAYED else f"first{g}"
        for d in (1, 3) if g in RELAYED else (1, 3, 2):
            send(event, "link", mine_b, mine_b, device(dy=d))
            send(event, "link", mine_c, mine_c, device(dx=d))

    def relay(g):
        need(f"near{g}")
        for half, sign in (("0", 1), ("1", -1)):
            oy = lax.rem(y + (4 - sign), 4)
            piece = own(group(g), "B" + half, x, lax.div(oy, 2), lax.rem(oy, 2), c)
            send(f"relay{g}", "link", piece, piece, device(dy=sign))
            piece = own(group(g), "C" + half, lax.rem(x + (4 - sign), 4), yh, yl, c)
            send(f"relay{g}", "link", piece, piece, device(dx=sign))

    def second_axis(g):
        if g in RELAYED:
            need(f"near{g}", f"relay{g}")
        else:
            need(f"first{g}")
        row = own(group(g), "B", x, slice(None), slice(None), c)
        column = own(group(g), "C", slice(None), yh, yl, c)
        for sign in (1, -1):
            send(f"bx{g}{sign}", "link", row, row, device(dx=sign))
            send(f"cy{g}{sign}", "link", column, column, device(dy=sign))

    def far(g):
        for i, sign in enumerate((1, -1)):
            need(f"bx{g}{sign}")
            line = own(group(g), "B", lax.rem(x + (4 - sign), 4), i, slice(None), c)
            send(f"far{g}", "link", line, line, device(dx=sign))
            need(f"cy{g}{sign}")
            oy = lax.rem(y + (4 - sign), 4)
            line = own(group(g), "C", pl.ds(2 * i, 2), lax.div(oy, 2), lax.rem(oy, 2), c)
            send(f"far{g}", "link", line, line, device(dy=sign))

    def plane_a():
        mine = own(0, "A", x, yh, yl, c)
        for dx in range(4):
            for dy in range(4):
                if dx or dy:
                    send("ap", "ap", mine, mine, device(dx=dx, dy=dy))

    def ring_a(s, h):
        place = (pl.ds(2 * h, 2), slice(None), slice(None), c)
        for sign in ring_signs(s, h):
            need("ap" if s == 1 else f"az{s - 1}{h}{sign}")
            send(
                f"az{s}{h}{sign}",
                "az",
                own(SLOT[-sign * (s - 1)], "A", *place),
                own(SLOT[-sign * s], "A", *place),
                device(dz=sign),
            )

    def own_a(g):
        if g == 0:
            need("ap")
        else:
            need(*[f"az{g}{h}{sign}" for h in range(2) for sign in ring_signs(g, h)])

    def share_near(g):
        for d in (0, 1, 3):
            line = own(group(g), "B", lax.rem(x + d, 4), slice(None), slice(None), c)
            send(f"core{g}", "core", line, line, device(dc=1))
            oy = lax.rem(y + d, 4)
            line = own(group(g), "C", slice(None), lax.div(oy, 2), lax.rem(oy, 2), c)
            send(f"core{g}", "core", line, line, device(dc=1))

    def share_far(g):
        need(f"far{g}")
        line = own(group(g), "B", lax.rem(x + 2, 4), slice(None), slice(None), c)
        send(f"core{g}", "core", line, line, device(dc=1))
        oy = lax.rem(y + 2, 4)
        line = own(group(g), "C", slice(None), lax.div(oy, 2), lax.rem(oy, 2), c)
        send(f"core{g}", "core", line, line, device(dc=1))

    def share_a(g):
        own_a(g)
        block = own(group(g), "A", slice(None), slice(None), slice(None), c)
        send(f"core{g}", "core", block, block, device(dc=1))

    def weigh():
        need("exp")

        def body(t, _):
            inverse = 1.0 / expected[t] / (8.0 * ROWS)
            mine = panels[0, lax.div(t, 2), lax.rem(t, 2), yl, c].astype(jnp.float32)
            for k in range(8):
                weights[t, pl.ds(k * OWN, OWN), :] = (mine * inverse[k : k + 1, :]).astype(
                    jnp.bfloat16
                )
            return 0

        lax.fori_loop(0, 8, body, 0)

    def multiply(i):
        for slot in slots(i):
            need(f"core{GROUP_OF[slot]}")
        out_ref[:, i * WIDE : (i + 1) * WIDE] = product(weights, panels, i)

    along_z(1)
    first_axis(0)
    plane_a()
    along_z(2)
    along_z(3)
    along_z(4)
    first_axis(1)
    second_axis(0)
    first_axis(2)
    first_axis(3)
    ring_a(1, 0)
    ring_a(1, 1)
    first_axis(4)
    second_axis(1)
    far(0)
    share_near(0)
    share_a(0)
    relay(3)
    second_axis(2)
    relay(4)
    ring_a(2, 0)
    ring_a(2, 1)
    far(1)
    second_axis(3)
    share_near(1)
    share_far(0)
    share_a(1)
    weigh()
    ring_a(3, 0)
    far(2)
    second_axis(4)
    share_near(2)
    share_far(1)
    ring_a(3, 1)
    far(3)
    ring_a(4, 0)
    share_near(3)
    share_a(2)
    multiply(0)
    share_far(2)
    far(4)
    ring_a(4, 1)
    share_near(4)
    share_a(3)
    multiply(1)
    share_far(3)
    multiply(2)
    share_far(4)
    share_a(4)
    multiply(3)
    for g in range(5):
        need(f"core{g}")
    for d, i in DEPARTURES.items():
        semaphore = send_sem.at[i]
        if d == "exp":
            empty(semaphore, expected.at[pl.ds(0, 7)])
        elif d == "ap":
            empty(semaphore, rows(480))
        elif d == "z":
            empty(semaphore, rows(448))
        elif d == "az":
            empty(semaphore, rows(3584))
        elif d == "link":
            empty(semaphore, panels.at[pl.ds(0, 5), :, :, :, 0])
        elif d == "core":
            empty(semaphore, panels.at[pl.ds(0, 4)])
        else:
            departed[d].wait_send()


def local(
    derivative,
    group_ids,
    group_scale,
    plane_coupling,
    band_second,
    band_third,
    band_offset,
    band_width,
    expected,
):
    flat = derivative.reshape(2 * CELLS, OWN)
    every = expected.transpose(1, 2, 3, 4, 0).reshape(ROWS, 64)
    hbm = pl.BlockSpec(memory_space=pltpu.HBM)
    vmem = pl.BlockSpec(memory_space=pltpu.VMEM)
    made = pl.pallas_call(
        kernel,
        out_shape=[
            pltpu.VMEM((8, 4, 2, 2, 2, OWN, ROWS), jnp.bfloat16),
            pltpu.VMEM((8, 8 * OWN, ROWS), jnp.bfloat16),
            pltpu.VMEM((8 * OWN, HEAD), jnp.float32),
        ],
        in_specs=[hbm] * 9,
        out_specs=[vmem] * 3,
        scratch_shapes=[
            pltpu.VMEM((2, CELLS, OWN), jnp.bfloat16),
            pltpu.VMEM((8, 8, ROWS), jnp.float32),
            pltpu.VMEM((2 * CELLS, OWN), jnp.bfloat16),
            pltpu.VMEM((1, OWN), jnp.int32),
            pltpu.SMEM((8,), jnp.float32),
            pltpu.SMEM((2, 2), jnp.float32),
            pltpu.SMEM((3, 4), jnp.float32),
            pltpu.SMEM((3, 4), jnp.float32),
            pltpu.SMEM((8,), jnp.int32),
            pltpu.SMEM((8,), jnp.int32),
            pltpu.VMEM((ROWS, 64), jnp.float32),
            pltpu.VMEM((64, ROWS), jnp.float32),
            pltpu.VMEM((CELLS, CELLS), jnp.float32),
            pltpu.VMEM((1, OWN), jnp.float32),
            pltpu.SemaphoreType.DMA((9,)),
            pltpu.SemaphoreType.DMA((len(DEPARTURES),)),
            pltpu.SemaphoreType.DMA((len(EVENTS),)),
        ],
        compiler_params=pltpu.CompilerParams(
            collective_id=0, has_side_effects=True, vmem_limit_bytes=16 * 1024 * 1024
        ),
        cost_estimate=pl.CostEstimate(
            flops=2 * 768 * 2048 * HEAD, bytes_accessed=10_000_000, transcendentals=0
        ),
        name="fisher",
    )(
        *[
            pltpu.with_memory_space_constraint(a, pltpu.HBM)
            for a in (
                flat,
                group_ids.reshape(1, OWN),
                group_scale,
                plane_coupling,
                band_second,
                band_third,
                band_offset,
                band_width,
                every,
            )
        ]
    )
    out = pl.pallas_call(
        finish,
        out_shape=jax.ShapeDtypeStruct((8 * OWN, 3072), jnp.float32),
        in_specs=[vmem] * 3,
        out_specs=hbm,
        scratch_shapes=[
            pltpu.VMEM((8 * OWN, 3072 - HEAD), jnp.float32),
            pltpu.SemaphoreType.DMA((8,)),
        ],
        compiler_params=pltpu.CompilerParams(vmem_limit_bytes=16 * 1024 * 1024),
        cost_estimate=pl.CostEstimate(
            flops=2 * 768 * 2048 * (3072 - HEAD), bytes_accessed=10_000_000, transcendentals=0
        ),
        name="finish",
    )(*[pltpu.with_memory_space_constraint(a, pltpu.VMEM) for a in made])
    return out.reshape(8, OWN, 3072)


def solution(mesh):
    placed = (
        P("bin", None, None, None, "nuis"),
        P("nuis"),
        P(),
        P(None, "bin"),
        P(),
        P(),
        P(),
        P(),
        P(None, "bin", None, None, None),
    )
    return jax.shard_map(
        local, mesh=mesh, in_specs=placed, out_specs=P("bin", "nuis", None), check_vma=False
    )
```
